256 devices in a mesh: dp: 8 (over y, core), table: 32 (over z, x).
Axes of the slice: x: 4, y: 4, z: 8, core: 2. Of those that a mesh axis runs over, the one named last changes fastest.
Arguments:
- queries: bfloat16 [32768, 768], P(('dp', 'table')), may hold values from -10.2 to 10.2
- tile_ids: int32 [32768, 4], P(('dp', 'table')), may hold values from 0 to 255, as said below
- knowledge: bfloat16 [256, 64, 768], P('table'), may hold values from -6 to 6
- out_proj: bfloat16 [768, 768], replicated, may hold values from -0.21875 to 0.21875
- labels: bfloat16 [64, 512, 768], P('table'), may hold values from -0.21875 to 0.21875
- cluster_ids: int32 [32768, 4], P(('dp', 'table')), may hold values from 0 to 63, all different within a row; in each aligned block of 128 rows (0 to 127, 128 to 255, ...) at most 16 rows name the same one
- positive_picks: int32 [32768, 4], P(('dp', 'table')), may hold values from 0 to 2047
Outputs:
- loss: float32 [32768], P(('dp', 'table'))
- query_grad: float32 [32768, 768], P(('dp', 'table'))
- knowledge_grad: float32 [256, 64, 768], P('table', 'dp')
- label_step: float32 [64, 512, 768], P('table', 'dp')
The draws below stay inside these ranges and needn't reach their ends.
Inputs may be any that keep to these rules, and one draw needn't show every extreme that they name: `tile_ids`: the queries of one device name at most one distinct tile of each table shard of 8 consecutive tiles; a query may name a tile more than once. `cluster_ids`: each row names 4 different clusters; within the rows of one device no cluster is named by more than 16 rows. `positive_picks`: entry j names label j % 512 of the cluster in column j // 512 of the same row of cluster_ids.
All inputs are finite; a program needn't handle non-finite values.
Results may differ from the reference program's by a relative error of at most 0.015.
Values may be sent and summed in bfloat16 or wider, within the bound.
A program may use at most 128 MiB of HBM per device.

```python
import math
import jax
import jax.numpy as jnp
import numpy as np
from jax import lax

D = 768
HEADS = 12
Q_DEV = 128
ARTICLE_PANES = 8
TROWS = 64
RETR = 4
SHORT = 4
LC = 512
NPOS = 4
QUERIES = 32768
TILES = 256
CLUSTERS = 64
MOST = 16


def draw_queries(key, part):
    key = jax.random.fold_in(key, 7)
    first, second = jax.random.split(key, 2)
    column = jnp.exp(jax.random.uniform(first, (1, D), minval=math.log(0.3), maxval=math.log(3.0)))
    values = jnp.clip(jax.random.normal(second, (QUERIES, D)), -3.4, 3.4) * column
    return values.astype(jnp.float32).astype(jnp.bfloat16)


def draw_tile_ids(key, part):
    key = jax.random.fold_in(key, 11)
    blocks = QUERIES // Q_DEV
    owners = TILES // ARTICLE_PANES
    first, second, third, fourth, fifth = jax.random.split(key, 5)
    level = jax.random.randint(first, (blocks, 1), 1, 5)
    chosen = jax.random.randint(second, (blocks, owners), 0, 4) < level
    forced = jax.random.randint(third, (blocks, 1), 0, owners)
    chosen = chosen | (jnp.arange(owners, dtype=jnp.int32)[None, :] == forced)
    local_tile = jax.random.randint(fourth, (blocks, owners), 0, ARTICLE_PANES)
    running = jnp.cumsum(chosen.astype(jnp.int32), axis=1)
    total_used = running[:, -1:]
    picked = jax.random.randint(fifth, (blocks, Q_DEV * RETR), 0, 1 << 30) % total_used
    owner = jnp.sum((running[:, None, :] <= picked[:, :, None]).astype(jnp.int32), axis=2)
    owner_local = jnp.take_along_axis(local_tile, owner, axis=1)
    tiles = owner * ARTICLE_PANES + owner_local
    return tiles.reshape(QUERIES, RETR).astype(jnp.int32)


def with_ends(result, rng, low, top_value):
    longest = result.shape.index(max(result.shape))
    spots = []
    for shift in (0, 1):
        where = [jax.random.randint(jax.random.fold_in(rng, axis), (), 0, length) for axis, length in enumerate(result.shape)]
        where[longest] = (where[longest] + shift) % result.shape[longest]
        spots.append(tuple(where))
    return result.at[spots[0]].set(low).at[spots[1]].set(top_value)


def block_levels(own_key, dims, cuts, smallest, top_value):
    level, own = 1.0, jax.random.fold_in(own_key, 6)
    for position, blocks in cuts:
        heights = jnp.exp(jax.random.uniform(jax.random.fold_in(own, position), (blocks,), jnp.float32, smallest / len(cuts), top_value / len(cuts)))
        level = level * jnp.repeat(heights, dims[position] // blocks).reshape([-1 if axis == position else 1 for axis in range(len(dims))])
    return level


def assign_block(stream_key, own, number, rows, amount, top, reach, skew):
    order = jax.random.permutation(stream_key, amount)
    crowded, ordinary = load_shares(amount, rows * top, reach, skew, True), load_shares(amount, rows * top, reach, skew, False)
    places = jnp.arange(amount)

    def named(tallies, rotation):
        used = int((tallies > 0).sum())
        fixed = max(1, used // 4)
        passed = fixed + (places - fixed + rotation * (used - fixed)) % max(1, amount - fixed)
        return jnp.zeros((amount,), jnp.int32).at[order[jnp.where(places < fixed, places, passed)]].set(jnp.asarray(tallies, jnp.int32))

    tallies = jnp.where(number % 4 == 0, named(crowded, number // 4), named(ordinary, number - number // 4 - 1))
    mixed = jax.random.permutation(jax.random.fold_in(own, 3), amount)
    giver, receiver = mixed[0:amount // 2 * 2:2], mixed[1:amount // 2 * 2:2]
    slack = jnp.minimum(tallies[giver] - 1, reach - tallies[receiver]) // 2
    slack = jnp.where((giver == order[0]) | (receiver == order[0]) | (tallies[receiver] == 0), 0, jnp.maximum(slack, 0))
    passed = jax.random.randint(jax.random.fold_in(own, 4), (amount // 2,), 0, 1 << 20) % (slack + 1)
    tallies = tallies.at[giver].add(-passed).at[receiver].add(passed)
    members = jnp.searchsorted(jnp.cumsum(tallies), jnp.arange(rows * top), side="right").astype(jnp.int32)
    grid = members.reshape(top, rows).T
    grid = grid[jax.random.permutation(jax.random.fold_in(own, 1), rows)]
    rotation = jax.random.randint(jax.random.fold_in(own, 2), (rows, 1), 0, top)
    return jnp.take_along_axis(grid, (jnp.arange(top)[None, :] + rotation) % top, axis=1)


def load_shares(number_of, total, limit, slope, full):
    loads = [(1 << 20) // math.isqrt(rank ** slope) + 1 for rank in range(1, number_of + 1)]
    largest = limit if full else min(limit, max(-(-total // number_of), total * loads[0] // sum(loads)))
    least = 1 if total - largest >= number_of - 1 else 0
    counts, rest = [largest] + [least] * (number_of - 1), total - largest - least * (number_of - 1)
    while rest > 0:
        movable = [i for i in range(1, number_of) if counts[i] < largest] or [i for i in range(1, number_of) if counts[i] < limit]
        mass, left = sum([loads[i] for i in movable]), rest
        for i in movable:
            more = min(limit - counts[i], max(1, left * loads[i] // mass), rest)
            counts[i] = counts[i] + more
            rest = rest - more
    return np.array(counts)


def scatter_about(key, dims, width, most, cuts=(), held_as=jnp.bfloat16):
    values = jax.random.normal(key, dims, jnp.float32) * width
    if len(cuts) > 0:
        values = block_levels(key, dims, cuts, -0.22, 0.18) * values
    return jnp.clip(values, min=-most, max=most).astype(held_as)


def setup_inputs(seed: int = 0) -> dict:
    arg_keys = jax.random.split(jax.random.key(seed), 8)
    queries = draw_queries(jax.random.fold_in(arg_keys[7], 71), 0)
    tile_ids = draw_tile_ids(jax.random.fold_in(arg_keys[7], 71), 0)
    knowledge = scatter_about(arg_keys[2], (TILES, TROWS, D), 1.0, 6.0, ((0, 32),))
    out_proj = scatter_about(arg_keys[3], (D, D), D ** -0.5, 0.21875)
    labels = scatter_about(arg_keys[4], (CLUSTERS, LC, D), D ** -0.5, 0.21875, ((0, 32),))
    cluster_ids_keys = jax.random.split(jax.random.fold_in(arg_keys[5], 1), QUERIES // Q_DEV)
    cluster_ids_turns = jax.random.permutation(jax.random.fold_in(arg_keys[5], 3), QUERIES // Q_DEV)
    cluster_ids = jax.vmap(lambda own, number: assign_block(jax.random.fold_in(arg_keys[5], 2), own, number, Q_DEV, CLUSTERS, SHORT, MOST, 2))(cluster_ids_keys, cluster_ids_turns).reshape((QUERIES, SHORT))
    positive_picks = with_ends(jax.random.randint(arg_keys[6], (QUERIES, NPOS), 0, SHORT * LC), jax.random.fold_in(arg_keys[6], 1), 0, (SHORT * LC) - 1).astype(jnp.int32)
    return dict(queries=queries, tile_ids=tile_ids, knowledge=knowledge, out_proj=out_proj, labels=labels, cluster_ids=cluster_ids, positive_picks=positive_picks)


logit_ceiling = 10.0
epsilon = 1e-06

def widen(value):
    return lax.optimization_barrier(value).astype(jnp.float32)

def gather_keys(knowledge, id_rows):
    key_rows = knowledge[id_rows].reshape(Q_DEV, RETR * TROWS, D)
    same_tile = id_rows[:, :, None] == id_rows[:, None, :]
    multiple = lax.optimization_barrier(jnp.sum(same_tile.astype(jnp.float32), axis=2))
    order = jnp.arange(RETR, dtype=jnp.int32)
    earlier = jnp.any(same_tile & (order[None, None, :] < order[None, :, None]), axis=2)
    key_weight = jnp.where(earlier, jnp.zeros((), jnp.float32), multiple)
    return (key_rows, jnp.repeat(key_weight, TROWS, axis=1))

def attention(query_rows, key_rows, key_weight):
    head_size = D // HEADS
    query_head_rows = query_rows.astype(jnp.float32).reshape(Q_DEV, HEADS, head_size)
    lookup_facet_vectors = key_rows.astype(jnp.float32).reshape(Q_DEV, RETR * TROWS, HEADS, head_size)
    scores = jnp.einsum('bhd,bmhd->bhm', query_head_rows, lookup_facet_vectors) / math.sqrt(head_size)
    capped = jnp.tanh(scores / logit_ceiling)
    raw_weight = key_weight[:, None, :] * jnp.exp(logit_ceiling * capped)
    soft_weight = raw_weight / lax.optimization_barrier(jnp.sum(raw_weight, axis=2, keepdims=True))
    smoothed_lower_limit = soft_weight.astype(jnp.bfloat16)
    mixed_heads = jnp.einsum('bhm,bmhd->bhd', widen(smoothed_lower_limit), lookup_facet_vectors)
    mixed_rows = mixed_heads.reshape(Q_DEV, D).astype(jnp.bfloat16)
    return (mixed_rows, soft_weight, smoothed_lower_limit, capped, query_head_rows, lookup_facet_vectors)

def reference(queries, tile_ids, knowledge, out_proj, labels, cluster_ids, positive_picks):
    blocks = QUERIES // Q_DEV
    head_size = D // HEADS
    query_blocks = queries.reshape(blocks, Q_DEV, D)
    tile_blocks = tile_ids.reshape(blocks, Q_DEV, RETR)

    def forward(packed):
        query_rows, id_rows = packed
        key_rows, key_weight = gather_keys(knowledge, id_rows)
        mixed_rows = attention(query_rows, key_rows, key_weight)[0]
        lifted = query_rows.astype(jnp.float32) + jnp.dot(mixed_rows, out_proj, preferred_element_type=jnp.float32)
        return lifted.astype(jnp.bfloat16)
    augmented = lax.map(forward, (query_blocks, tile_blocks)).reshape(QUERIES, D)
    pair_count = QUERIES * SHORT
    capacity = MOST * blocks
    flat_cluster = cluster_ids.reshape(pair_count)
    member = (flat_cluster[:, None] == jnp.arange(CLUSTERS, dtype=jnp.int32)[None, :]).astype(jnp.int32)
    ordinal_entering = lax.optimization_barrier(jnp.sum(jnp.cumsum(member, axis=0) * member, axis=1)) - 1
    slot_of = flat_cluster * capacity + ordinal_entering
    source = jnp.zeros((CLUSTERS * capacity,), jnp.int32).at[slot_of].set(jnp.arange(pair_count, dtype=jnp.int32))
    filled = jnp.zeros((CLUSTERS * capacity,), jnp.float32).at[slot_of].set(1.0)
    label_grid = jnp.arange(LC, dtype=jnp.int32)

    def cluster_work(carry, cluster):
        d_augment, loss_total = carry
        couple_position = lax.dynamic_slice_in_dim(source, cluster * capacity, capacity)
        live_mask = lax.dynamic_slice_in_dim(filled, cluster * capacity, capacity)
        query_index = couple_position // SHORT
        cohort_entries = jnp.where(live_mask[:, None] > 0, augmented[query_index], jnp.zeros((), jnp.bfloat16))
        pick_ids = positive_picks[query_index]
        wanted_label = jnp.where(pick_ids // LC == (couple_position % SHORT)[:, None], pick_ids % LC, -1)
        target = jnp.any(wanted_label[:, :, None] == label_grid[None, None, :], axis=1).astype(jnp.float32)
        weight_rows = lax.dynamic_index_in_dim(labels, cluster, 0, keepdims=False)
        logits = jnp.dot(cohort_entries, weight_rows.T, preferred_element_type=jnp.float32)
        pair_loss = (lax.optimization_barrier(jnp.sum(jnp.log1p(jnp.exp(logits)) - target * logits, axis=1)) * live_mask).astype(jnp.bfloat16)
        d_logit = ((jax.nn.sigmoid(logits) - target) * live_mask[:, None]).astype(jnp.bfloat16)
        d_pair = jnp.dot(d_logit, weight_rows, preferred_element_type=jnp.float32).astype(jnp.bfloat16)
        grad_rows = jnp.dot(d_logit.T, cohort_entries, preferred_element_type=jnp.float32)
        d_augment = d_augment.at[query_index].add(widen(d_pair) * live_mask[:, None])
        loss_total = loss_total.at[query_index].add(widen(pair_loss) * live_mask)
        return ((d_augment, loss_total), grad_rows)
    start = (jnp.zeros((QUERIES, D), jnp.float32), jnp.zeros((QUERIES,), jnp.float32))
    (d_augment, loss_total), label_grad = lax.scan(cluster_work, start, jnp.arange(CLUSTERS, dtype=jnp.int32))
    loss = loss_total / (SHORT * LC)
    label_step = label_grad * lax.rsqrt(lax.optimization_barrier(jnp.mean(label_grad * label_grad, axis=2, keepdims=True)) + epsilon)

    def backward(carry, packed):
        query_rows, id_rows, d_rows_in = packed
        key_rows, key_weight = gather_keys(knowledge, id_rows)
        outcome = attention(query_rows, key_rows, key_weight)
        soft_weight, smoothed_lower_limit, capped, query_head_rows, lookup_facet_vectors = (outcome[1], outcome[2], outcome[3], outcome[4], outcome[5])
        back_proj = jnp.dot(d_rows_in.astype(jnp.bfloat16), out_proj.T, preferred_element_type=jnp.float32).astype(jnp.bfloat16)
        returned_heads = widen(back_proj).reshape(Q_DEV, HEADS, head_size)
        weight_gradient = jnp.einsum('bhd,bmhd->bhm', returned_heads, lookup_facet_vectors)
        d_capped = soft_weight * (weight_gradient - lax.optimization_barrier(jnp.sum(soft_weight * weight_gradient, axis=2, keepdims=True)))
        logit_derivative = widen((d_capped * (1.0 - capped * capped) / math.sqrt(head_size)).astype(jnp.bfloat16))
        d_query = jnp.einsum('bhm,bmhd->bhd', logit_derivative, lookup_facet_vectors).reshape(Q_DEV, D)
        key_gradient = jnp.einsum('bhm,bhd->bmhd', logit_derivative, query_head_rows) + jnp.einsum('bhm,bhd->bmhd', widen(smoothed_lower_limit), returned_heads)
        key_gradient = key_gradient.reshape(Q_DEV, RETR, TROWS, D)
        block_sum = jnp.zeros((TILES, TROWS, D), jnp.float32).at[id_rows].add(key_gradient)
        return (carry + widen(block_sum.astype(jnp.bfloat16)), d_rows_in + d_query)
    d_blocks = d_augment.reshape(blocks, Q_DEV, D)
    knowledge_grad, query_grad = lax.scan(backward, jnp.zeros((TILES, TROWS, D), jnp.float32), (query_blocks, tile_blocks, d_blocks))
    return (loss, query_grad.reshape(QUERIES, D), knowledge_grad, label_step)
```

```python
import functools
import math

import jax
import jax.numpy as jnp
from jax import lax
from jax.experimental import pallas as pl
from jax.experimental.pallas import tpu as pltpu
from jax.sharding import PartitionSpec as P

MESH = pl.DeviceIdType.MESH
DMA = pltpu.SemaphoreType.DMA
F32 = jnp.float32
BF16 = jnp.bfloat16
HEADS = 12
PAIRS = 6
Q = 128
D = 768
NZ = 8
NX = 4
NY = 4
epsilon = 1e-06
LOG2E = 1.4426950408889634
VMEM_LIMIT = 50 << 20


def where_am_i():
    dp, t = lax.axis_index("dp"), lax.axis_index("table")
    return dp // 2, dp % 2, t // NX, t % NX


def dev(y, c, z, x):
    return (y * 2 + c, z * NX + x)


def greet(peers):
    barrier = pltpu.get_barrier_semaphore()
    for peer in peers:
        pl.semaphore_signal(barrier, inc=1, device_id=peer, device_id_type=MESH)
    pl.semaphore_wait(barrier, len(peers))


def remote(src, dst, send, recv, to):
    return pltpu.make_async_remote_copy(
        src_ref=src, dst_ref=dst, send_sem=send, recv_sem=recv, device_id=to, device_id_type=MESH
    )


def nt(a, b):
    return lax.dot_general(a, b, (((1,), (1,)), ((), ())), preferred_element_type=F32)


def tn(a, b):
    return lax.dot_general(a, b, (((0,), (0,)), ((), ())), preferred_element_type=F32)


def nn(a, b):
    return jnp.dot(a, b, preferred_element_type=F32)


def stack_heads(rows, stacked_ref):
    lane = lax.broadcasted_iota(jnp.int32, (Q, 128), 1)
    for p in range(PAIRS):
        part = rows[:, p * 128 : (p + 1) * 128]
        stacked_ref[p, :Q] = jnp.where(lane < 64, part, jnp.zeros_like(part))
        stacked_ref[p, Q:] = jnp.where(lane < 64, jnp.zeros_like(part), part)


def unstack_heads(both):
    return jnp.concatenate([both[0:64, 0:Q], both[64:128, Q : 2 * Q]], axis=0)


def weight_block(tw):
    tw2 = jnp.concatenate([tw, tw], axis=1)
    return jnp.broadcast_to(tw2[:, None, :], (NX, 64, 2 * Q)).reshape(NX * 64, 2 * Q)


XC = [(dx, dc) for dx in range(NX) for dc in range(2)]


def keys_kernel(
    know, wanted, queries, tile_weight, out_proj, msg,
    keys, aug, mixed_t, total, asks, ints,
    half, r0, r1, r2, l0, l1, l2, far, stage, stacked, acc, mid,
    ask_smem, z_send, z_recv, x_send, x_recv, a_send, a_recv, m_send, m_recv, n_send, n_recv, l_sem,
):
    y, c, z, x = where_am_i()
    me = x * 2 + c
    right, left = dev(y, c, (z + 1) % NZ, x), dev(y, c, (z + NZ - 1) % NZ, x)
    group = [((x + dx) % NX, (c + dc) % 2) for dx, dc in XC]
    greet(
        [dev(y, pc, z, px) for px, pc in group[1:]]
        + [dev(y, c, (z + d) % NZ, x) for d in range(1, NZ)]
    )
    half[...] = know[:, pl.ds(pl.multiple_of(c * 32, 32), 32), :]
    ask_copies = []
    for j in range(1, 8):
        px, pc = group[j]
        cp = remote(wanted, asks.at[me], a_send.at[j], a_recv.at[j], dev(y, pc, z, px))
        cp.start()
        ask_copies.append(cp)
    ring = {}
    slots = ((half, r0, r1, r2, far), (half, l0, l1, l2, far))

    def ring_send(way, step, k):
        piece = pl.ds(k * 2, 2)
        cp = remote(
            slots[way][step].at[piece], slots[way][step + 1].at[piece],
            z_send.at[way, step, k], z_recv.at[way, step, k], right if way == 0 else left,
        )
        cp.start()
        ring[way, step, k] = cp

    for k in range(4):
        for way in (0, 1):
            ring_send(way, 0, k)
    m_copies = []
    for dx in range(1, NX):
        px = (x + dx) % NX
        cp = remote(msg.at[px], mid.at[x], m_send.at[dx], m_recv.at[dx], dev(y, c, z, px))
        cp.start()
        m_copies.append(cp)
    asks[me] = wanted[...]
    mid[x] = msg[x]
    stack_heads(queries[...], stacked)
    acc[...] = jnp.zeros_like(acc)
    total[...] = jnp.zeros_like(total)
    for cp in ask_copies:
        cp.wait()
    cp = pltpu.make_async_copy(asks, ask_smem, l_sem)
    cp.start()
    cp.wait()
    sent = []

    def serve(zo, shard):
        row = pl.ds(pl.multiple_of(c * 32, 32), 32)
        for j, (px, pc) in enumerate(group):
            tile = ask_smem[px * 2 + pc, zo, x]
            if j == 0:
                keys[zo * NX + x, row] = shard[tile]
                continue
            stage[j, zo] = shard[tile]
            cp = remote(
                stage.at[j, zo], keys.at[zo * NX + x, row], x_send.at[j, zo], x_recv.at[j, zo],
                dev(y, pc, z, px),
            )
            cp.start()
            sent.append(cp)

    def arrived(zo):
        for j in range(1, 8):
            row = pl.ds(0, 32)
            remote(
                stage.at[j, zo], keys.at[zo * NX, row], x_send.at[j, zo], x_recv.at[j, zo], right
            ).wait_recv()

    def attend(zo):
        w = weight_block(tile_weight[zo])

        def pair(p, carry):
            lanes = pl.ds(pl.multiple_of(p * 128, 128), 128)
            k = keys[pl.ds(zo * NX, NX), :, lanes].reshape(256, 128)
            capped = jnp.tanh(nt(k, stacked[p]) * (1.0 / 80.0))
            raw = w * jnp.exp2(capped * (10.0 * LOG2E))
            total[p] = total[p] + jnp.sum(raw, axis=0, keepdims=True)
            acc[p] = acc[p] + tn(k, raw.astype(BF16))
            return carry

        lax.fori_loop(0, PAIRS, pair, 0)

    def wait_step(way, step, k):
        ring[way, step, k].wait_recv()

    serve(z, half)
    for cp in m_copies:
        cp.wait()
    n_copies = []
    for d in range(1, NZ):
        zp = (z + d) % NZ
        cp = remote(
            mid.at[:, zp], ints.at[z], n_send.at[d], n_recv.at[d], dev(y, c, zp, x)
        )
        cp.start()
        n_copies.append(cp)
    ints[z] = mid[:, z]
    pending = [z]
    for step in range(1, 4):
        for k in range(4):
            for way in (0, 1):
                wait_step(way, step - 1, k)
                if step < 3 or (k < 2) == (way == 0):
                    ring_send(way, step, k)
        serve((z + NZ - step) % NZ, slots[0][step])
        serve((z + step) % NZ, slots[1][step])
        for zo in pending:
            arrived(zo)
            attend(zo)
        pending = [(z + NZ - step) % NZ, (z + step) % NZ]
    for k in range(4):
        wait_step(0 if k < 2 else 1, 3, k)
    serve((z + 4) % NZ, far)
    for zo in pending:
        arrived(zo)
        attend(zo)
    for cp in n_copies:
        cp.wait()
    arrived((z + 4) % NZ)
    attend((z + 4) % NZ)
    for p in range(PAIRS):
        mixed_t[p] = unstack_heads(acc[p] / total[p])
    mixed = jnp.concatenate([mixed_t[p].T for p in range(PAIRS)], axis=1).astype(BF16)
    aug[...] = (queries[...].astype(F32) + nn(mixed, out_proj[...])).astype(BF16)
    for cp in ring.values():
        cp.wait_send()
    for cp in sent:
        cp.wait_send()


def labels_kernel(
    aug, ints, wcol, labels,
    d_aug, loss, label_grad,
    rows, served, got, back, back_got, lstage, lgot, dlogit, onehot, lpart, lsend, lrecv,
    psend, prbuf,
    z_send, z_recv, x_send, x_recv, b_send, b_recv, s_send, s_recv, p_send, p_recv, q_send, q_recv,
):
    y, c, z, x = where_am_i()
    right, left = dev(y, c, (z + 1) % NZ, x), dev(y, c, (z + NZ - 1) % NZ, x)
    greet(
        [dev(y, c, z, (x + dx) % NX) for dx in range(1, NX)]
        + [dev(y, c, (z + d) % NZ, x) for d in range(1, NZ)]
    )
    ring = {}

    def ring_send(way, step, k):
        own = (z + NZ - step) % NZ if way == 0 else (z + step) % NZ
        piece = pl.ds(k * 32, 32)
        src = aug.at[piece] if step == 0 else rows.at[own, piece]
        cp = remote(
            src, rows.at[own, piece], z_send.at[way, step, k], z_recv.at[way, step, k],
            right if way == 0 else left,
        )
        cp.start()
        ring[way, step, k] = cp

    for k in range(4):
        for way in (0, 1):
            ring_send(way, 0, k)
    rows[z] = aug[...]
    query = lax.broadcasted_iota(jnp.int32, (Q, 128), 0)

    def hot(i, carry):
        onehot[i] = jnp.where(query == ints[i, x, 5:6, :], 1.0, 0.0).astype(BF16)
        return carry

    lax.fori_loop(0, NZ, hot, 0)
    sent = []

    def serve(zs):
        picked = tn(onehot[zs], rows[zs]).astype(BF16)
        served[zs] = picked.reshape(NX, 2, 16, D)
        got[x, :, zs] = served[zs, x]
        for dx in range(1, NX):
            px = (x + dx) % NX
            cp = remote(
                served.at[zs, px], got.at[x, :, zs], x_send.at[dx, zs], x_recv.at[dx, zs],
                dev(y, c, z, px),
            )
            cp.start()
            sent.append(cp)

    serve(z)
    for step in range(1, 4):
        for k in range(4):
            for way in (0, 1):
                ring[way, step - 1, k].wait_recv()
                if step < 3 or (k < 2) == (way == 0):
                    ring_send(way, step, k)
        serve((z + NZ - step) % NZ)
        serve((z + step) % NZ)
    for k in range(4):
        ring[0 if k < 2 else 1, 3, k].wait_recv()
    serve((z + 4) % NZ)
    label = lax.broadcasted_iota(jnp.int32, (128, 512), 1)
    lane = lax.broadcasted_iota(jnp.int32, (NZ, 16, 128), 2)
    source = lax.broadcasted_iota(jnp.int32, (NZ, 16, 128), 0)

    def work(xs):
        def cluster(cl, carry):
            entries = got[xs, cl].reshape(128, D)
            logits = nt(entries, labels[cl])
            want = wcol[xs * 2 + cl]
            live = (want[:, 4:5] > 0).astype(F32)
            hit = label == want[:, 0:1]
            for j in range(1, 4):
                hit = hit | (label == want[:, j : j + 1])
            e = jnp.exp(-jnp.abs(logits))
            soft = jnp.maximum(logits, 0.0) + jnp.log1p(e)
            pair_loss = jnp.sum(soft - jnp.where(hit, logits, 0.0), axis=1, keepdims=True) * live
            inv = 1.0 / (1.0 + e)
            sig = jnp.where(logits >= 0, inv, 1.0 - inv)
            dl = ((sig - jnp.where(hit, 1.0, 0.0)) * live).astype(BF16)
            dlogit[cl, xs] = dl
            back[xs, cl] = nn(dl, labels[cl]).astype(BF16).reshape(NZ, 16, D)
            spread = jnp.broadcast_to(pair_loss, (128, 128)).reshape(NZ, 16, 128)
            lstage[xs, cl] = jnp.sum(jnp.where(lane == source, spread, 0.0), axis=0)
            return carry

        lax.fori_loop(0, 2, cluster, 0)

    back_copies = []
    for dx in (0, 1, 3, 2):
        xs = (x + NX - dx) % NX
        if dx:
            for zs in range(NZ):
                remote(
                    served.at[0, 0], got.at[xs, :, 0], x_send.at[dx, zs], x_recv.at[dx, zs], right
                ).wait_recv()
        work(xs)
        if dx == 0:
            back_got[x] = back[x]
            lgot[x] = lstage[x]
        else:
            to = dev(y, c, z, xs)
            for cp in (
                remote(back.at[xs], back_got.at[x], b_send.at[dx], b_recv.at[dx], to),
                remote(lstage.at[xs], lgot.at[x], s_send.at[dx], s_recv.at[dx], to),
            ):
                cp.start()
                back_copies.append(cp)
    for cl in range(2):
        label_grad[cl] = tn(
            dlogit[cl].reshape(512, 512), got[:, cl].reshape(512, D)
        ).astype(BF16)
    for cp in back_copies:
        cp.wait()

    def partial(zs):
        pairs = back_got[:, :, zs].reshape(128, D)
        return nn(onehot[zs], pairs)

    p_copies = []

    def chain_send(way, step, value, dest_rows):
        psend[way, step, dest_rows] = value.astype(BF16)
        cp = remote(
            psend.at[way, step, dest_rows], prbuf.at[way, step, dest_rows],
            p_send.at[way, step], p_recv.at[way, step], right if way == 0 else left,
        )
        cp.start()
        p_copies.append(cp)
        return cp

    low, high, whole = pl.ds(0, 64), pl.ds(64, 64), pl.ds(0, Q)
    far = partial((z + 4) % NZ)
    previous = [chain_send(0, 0, far[:64], low), chain_send(1, 0, far[64:], high)]
    losses = jnp.concatenate([lgot[i].reshape(32, 128) for i in range(NX)], axis=0).astype(BF16)
    out_lane = lax.broadcasted_iota(jnp.int32, (Q, 128), 1)
    lpart[...] = jnp.zeros_like(lpart)

    def loss_of(i, carry):
        lpart[...] = lpart[...] + jnp.where(out_lane == i, nn(onehot[i], losses), 0.0)
        return carry

    lax.fori_loop(0, NZ, loss_of, 0)
    lsend[...] = lpart[...].T[:NZ]
    l_copies = []
    for d in range(1, NZ):
        zp = (z + d) % NZ
        cp = remote(lsend, lrecv.at[z], q_send.at[d], q_recv.at[d], dev(y, c, zp, x))
        cp.start()
        l_copies.append(cp)
    lrecv[z] = lsend[...]
    for step in range(1, 4):
        d = 4 - step
        to_right, to_left = partial((z + d) % NZ), partial((z + NZ - d) % NZ)
        for cp in previous:
            cp.wait_recv()
        if step == 1:
            zeros = jnp.zeros((64, D), F32)
            in_right = jnp.concatenate([prbuf[0, 0, :64].astype(F32), zeros], axis=0)
            in_left = jnp.concatenate([zeros, prbuf[1, 0, 64:].astype(F32)], axis=0)
        else:
            in_right, in_left = prbuf[0, step - 1].astype(F32), prbuf[1, step - 1].astype(F32)
        previous = [
            chain_send(0, step, to_right + in_right, whole),
            chain_send(1, step, to_left + in_left, whole),
        ]
    mine = partial(z)
    for cp in previous:
        cp.wait_recv()
    d_aug[...] = mine + prbuf[0, 3].astype(F32) + prbuf[1, 3].astype(F32)
    for cp in l_copies:
        cp.wait()
    loss[...] = jnp.sum(lrecv[:, pl.ds(z, 1), :], axis=0) * (1.0 / 2048.0)
    for cp in p_copies:
        cp.wait_send()
    for cp in ring.values():
        cp.wait_send()
    for cp in sent:
        cp.wait_send()


def grads_kernel(
    asks, keys, queries, d_aug, out_proj, mixed_t, total, tile_weight,
    query_grad, know_grad,
    stacked, d_acc, delta, gsend, ggot, ysend, ygot, zsend, zgot,
    x_send, x_recv, y_send, y_recv, z_send, z_recv,
):
    y, c, z, x = where_am_i()
    me = x * 2 + c
    group = [((x + dx) % NX, (c + dc) % 2) for dx, dc in XC]
    greet(
        [dev(y, pc, z, px) for px, pc in group[1:]]
        + [dev((y + d) % NY, c, z, x) for d in range(1, NY)]
        + [dev(y, c, (z + d) % NZ, x) for d in range(1, NZ)]
    )
    d_rows = d_aug[...]
    back_proj = nt(d_rows.astype(BF16), out_proj[...]).astype(BF16)
    stack_heads(queries[...], stacked.at[:, 0:256])
    stack_heads(back_proj, stacked.at[:, 256:512])
    for p in range(PAIRS):
        product = mixed_t[p] * back_proj[:, p * 128 : (p + 1) * 128].astype(F32).T
        delta[p] = jnp.concatenate(
            [
                jnp.sum(product[:64], axis=0, keepdims=True),
                jnp.sum(product[64:], axis=0, keepdims=True),
            ],
            axis=1,
        )
    d_acc[...] = jnp.zeros_like(d_acc)

    def compute(zo):
        w = weight_block(tile_weight[zo])

        def pair(p, carry):
            lanes = pl.ds(pl.multiple_of(p * 128, 128), 128)
            k = keys[pl.ds(zo * NX, NX), :, lanes].reshape(256, 128)
            rows = stacked[p]
            products = nt(k, rows)
            capped = jnp.tanh(products[:, :256] * (1.0 / 80.0))
            soft = w * jnp.exp2(capped * (10.0 * LOG2E)) * (1.0 / total[p])
            d_score = soft * (products[:, 256:] - delta[p]) * ((1.0 - capped * capped) * 0.125)
            both = jnp.concatenate([d_score.astype(BF16), soft.astype(BF16)], axis=1)
            d_acc[p] = d_acc[p] + tn(k, both[:, :256])
            grad = nn(both, rows).reshape(NX, NY, 2, 8, 128)
            for side in range(2):
                gsend[zo, :, side, :, lanes] = grad[:, :, side].reshape(NX, 32, 128).astype(BF16)
            return carry

        lax.fori_loop(0, PAIRS, pair, 0)
        ggot[me, zo] = gsend[zo, x, c]
        for j in range(1, 8):
            px, pc = group[j]
            remote(
                gsend.at[zo, px, pc], ggot.at[me, zo], x_send.at[j, zo], x_recv.at[j, zo],
                dev(y, pc, z, px),
            ).start()

    def gather_tiles(zo):
        for j in range(1, 8):
            remote(
                gsend.at[zo, 0, 0], ggot.at[0, zo], x_send.at[j, zo], x_recv.at[j, zo],
                dev(y, c, z, x),
            ).wait_recv()
        tiles = [asks[s, zo, x] for s in range(8)]

        def two_tiles(k2, carry):
            sums = []
            for k in range(2):
                value = jnp.zeros((32, D), F32)
                for s in range(8):
                    value = value + ggot[s, zo].astype(F32) * jnp.where(
                        tiles[s] == k2 * 2 + k, 1.0, 0.0
                    )
                sums.append(value.reshape(NY, 1, 8, D))
            joined = jnp.concatenate(sums, axis=1).reshape(NY, 16, D).astype(BF16)
            ysend[zo, :, k2] = joined
            return carry

        lax.fori_loop(0, 4, two_tiles, 0)
        ygot[y, zo] = ysend[zo, y]
        for d in range(1, NY):
            py = (y + d) % NY
            remote(
                ysend.at[zo, py], ygot.at[y, zo], y_send.at[d, zo], y_recv.at[d, zo],
                dev(py, c, z, x),
            ).start()

    def gather_shards(zo, own):
        for d in range(1, NY):
            remote(
                ysend.at[zo, 0], ygot.at[0, zo], y_send.at[d, zo], y_recv.at[d, zo],
                dev(y, c, z, x),
            ).wait_recv()
        value = ygot[0, zo].astype(F32)
        for i in range(1, NY):
            value = value + ygot[i, zo].astype(F32)
        zsend[zo] = value.astype(BF16)

        @pl.when(own == 0)
        def _():
            zgot[z] = zsend[z]

        @pl.when(own != 0)
        def _():
            remote(
                zsend.at[zo], zgot.at[z], z_send.at[own], z_recv.at[own], dev(y, c, zo, x)
            ).start()

    def offset(i):
        return (3 * (i + 1)) % NZ

    def body(i, carry):
        @pl.when(i < 8)
        def _():
            compute((z + offset(i)) % NZ)

        @pl.when((i >= 1) & (i < 9))
        def _():
            gather_tiles((z + offset(i - 1)) % NZ)

        @pl.when(i >= 2)
        def _():
            gather_shards((z + offset(i - 2)) % NZ, offset(i - 2))

        return carry

    lax.fori_loop(0, 10, body, 0)
    d_query = jnp.concatenate([unstack_heads(d_acc[p]).T for p in range(PAIRS)], axis=1)
    query_grad[...] = d_rows + d_query
    for d in range(1, NZ):
        remote(zsend.at[0], zgot.at[0], z_send.at[d], z_recv.at[d], dev(y, c, z, x)).wait_recv()
    value = zgot[0].astype(F32)
    for i in range(1, NZ):
        value = value + zgot[i].astype(F32)
    know_grad[...] = value.reshape(8, 8, D)

    def drain(zo, carry):
        for j in range(1, 8):
            remote(
                gsend.at[zo, 0, 0], ggot.at[0, zo], x_send.at[j, zo], x_recv.at[j, zo],
                dev(y, c, z, x),
            ).wait_send()
        for d in range(1, NY):
            remote(
                ysend.at[zo, 0], ygot.at[0, zo], y_send.at[d, zo], y_recv.at[d, zo],
                dev(y, c, z, x),
            ).wait_send()
        return carry

    lax.fori_loop(0, NZ, drain, 0)
    for d in range(1, NZ):
        remote(zsend.at[0], zgot.at[0], z_send.at[d], z_recv.at[d], dev(y, c, z, x)).wait_send()


V = pl.BlockSpec(memory_space=pltpu.VMEM)
S = pl.BlockSpec(memory_space=pltpu.SMEM)


def run(kernel, number, outs, scratch, *args, in_specs=None):
    return pl.pallas_call(
        kernel,
        out_shape=[jax.ShapeDtypeStruct(shape, dtype) for shape, dtype in outs],
        in_specs=in_specs or [V] * len(args),
        out_specs=[V] * len(outs),
        scratch_shapes=scratch,
        compiler_params=pltpu.CompilerParams(
            collective_id=number, has_side_effects=True, vmem_limit_bytes=VMEM_LIMIT
        ),
        cost_estimate=pl.CostEstimate(
            flops=4_000_000_000, bytes_accessed=40_000_000, transcendentals=6_000_000
        ),
    )(*args)


def prepare(tile_ids, cluster_ids, positive_picks):
    tiles, ids, picks = tile_ids.T, cluster_ids.T, positive_picks.T
    owner = jnp.arange(32, dtype=jnp.int32)
    hits = (tiles // 8)[:, None, :] == owner[None, :, None]
    tile_weight = jnp.sum(hits.astype(F32), axis=0)
    wanted = jnp.max(jnp.where(hits, (tiles % 8)[:, None, :], 0), axis=(0, 2))
    wanted = jnp.pad(wanted.reshape(NZ, NX), ((0, 0), (0, 128 - NX)))
    cluster = jnp.arange(64, dtype=jnp.int32)
    member = jnp.any(ids[:, None, :] == cluster[None, :, None], axis=0)
    before = (jnp.arange(Q)[:, None] < jnp.arange(Q)[None, :]).astype(BF16)
    rank = jnp.dot(member.astype(BF16), before, preferred_element_type=F32).astype(jnp.int32)
    rank = jnp.where(member, rank, -1)
    slot = jnp.arange(16, dtype=jnp.int32)
    held = rank[:, None, :] == slot[None, :, None]
    query = jnp.arange(Q, dtype=jnp.int32)
    slot_query = Q + jnp.sum(jnp.where(held, query - Q, 0), axis=2)
    live = (slot_query < Q).astype(jnp.int32)
    column = picks // 512
    pick_cluster = jnp.sum(
        jnp.where(column[:, None, :] == jnp.arange(4)[None, :, None], ids[None], 0), axis=1
    )
    pick_label = picks % 512 + 1
    wanted_label = [
        jnp.sum(
            jnp.where(
                held & (pick_cluster[j][None, None, :] == cluster[:, None, None]),
                pick_label[j],
                0,
            ),
            axis=2,
        )
        - 1
        for j in range(4)
    ]
    parts = [a.reshape(NZ, NX, 1, 32) for a in wanted_label + [live]]
    parts = jnp.pad(jnp.concatenate(parts, axis=2), ((0, 0), (0, 0), (0, 0), (0, 96)))
    slots = jnp.broadcast_to(slot_query.reshape(NZ, 1, 1, 128), (NZ, NX, 1, 128))
    msg = jnp.concatenate([parts, slots, jnp.zeros((NZ, NX, 2, 128), jnp.int32)], axis=2)
    return tile_weight.reshape(NZ, NX, Q), wanted, msg.transpose(1, 0, 2, 3)


def on_device(queries, tile_ids, knowledge, out_proj, labels, cluster_ids, positive_picks):
    tile_weight, wanted, msg = prepare(tile_ids, cluster_ids, positive_picks)
    keys, aug, mixed_t, total, asks, ints = run(
        keys_kernel,
        1,
        [
            ((32, 64, D), BF16),
            ((Q, D), BF16),
            ((PAIRS, 128, Q), F32),
            ((PAIRS, 1, 2 * Q), F32),
            ((8, 8, 128), jnp.int32),
            ((NZ, NX, 8, 128), jnp.int32),
        ],
        [
            *[pltpu.VMEM((8, 32, D), BF16) for _ in range(8)],
            pltpu.VMEM((8, NZ, 32, D), BF16),
            pltpu.VMEM((PAIRS, 2 * Q, 128), BF16),
            pltpu.VMEM((PAIRS, 128, 2 * Q), F32),
            pltpu.VMEM((NX, NZ, 8, 128), jnp.int32),
            pltpu.SMEM((8, 8, 128), jnp.int32),
            DMA((2, 4, 4)),
            DMA((2, 4, 4)),
            DMA((8, NZ)),
            DMA((8, NZ)),
            DMA((8,)),
            DMA((8,)),
            DMA((NX,)),
            DMA((NX,)),
            DMA((NZ,)),
            DMA((NZ,)),
            DMA,
        ],
        knowledge, wanted, queries, tile_weight, out_proj, msg,
    )
    wcol = ints[:, :, :5, :32].reshape(NZ, NX, 5, 2, 16).transpose(1, 3, 0, 4, 2)
    wcol = jnp.pad(wcol.reshape(8, 128, 5), ((0, 0), (0, 0), (0, 3)))
    d_aug, loss, label_grad = run(
        labels_kernel,
        2,
        [((Q, D), F32), ((1, Q), F32), ((2, 512, D), BF16)],
        [
            pltpu.VMEM((NZ, Q, D), BF16),
            pltpu.VMEM((NZ, NX, 2, 16, D), BF16),
            pltpu.VMEM((NX, 2, NZ, 16, D), BF16),
            pltpu.VMEM((NX, 2, NZ, 16, D), BF16),
            pltpu.VMEM((NX, 2, NZ, 16, D), BF16),
            pltpu.VMEM((NX, 2, 16, 128), F32),
            pltpu.VMEM((NX, 2, 16, 128), F32),
            pltpu.VMEM((2, NX, 128, 512), BF16),
            pltpu.VMEM((NZ, Q, 128), BF16),
            pltpu.VMEM((Q, 128), F32),
            pltpu.VMEM((NZ, 128), F32),
            pltpu.VMEM((NZ, NZ, 128), F32),
            pltpu.VMEM((2, 4, Q, D), BF16),
            pltpu.VMEM((2, 4, Q, D), BF16),
            DMA((2, 4, 4)),
            DMA((2, 4, 4)),
            DMA((NX, NZ)),
            DMA((NX, NZ)),
            DMA((NX,)),
            DMA((NX,)),
            DMA((NX,)),
            DMA((NX,)),
            DMA((2, 4)),
            DMA((2, 4)),
            DMA((NZ,)),
            DMA((NZ,)),
        ],
        aug, ints, wcol, labels,
    )
    grad_share = lax.psum_scatter(label_grad, "dp", scatter_dimension=1, tiled=True).astype(F32)
    label_step = grad_share * lax.rsqrt(
        jnp.mean(grad_share * grad_share, axis=2, keepdims=True) + epsilon
    )
    query_grad, knowledge_grad = run(
        grads_kernel,
        3,
        [((Q, D), F32), ((8, 8, D), F32)],
        [
            pltpu.VMEM((PAIRS, 4 * Q, 128), BF16),
            pltpu.VMEM((PAIRS, 128, 2 * Q), F32),
            pltpu.VMEM((PAIRS, 1, 2 * Q), F32),
            pltpu.VMEM((NZ, NX, 2, 32, D), BF16),
            pltpu.VMEM((8, NZ, 32, D), BF16),
            pltpu.VMEM((NZ, NY, 4, 16, D), BF16),
            pltpu.VMEM((NY, NZ, 4, 16, D), BF16),
            pltpu.VMEM((NZ, 4, 16, D), BF16),
            pltpu.VMEM((NZ, 4, 16, D), BF16),
            DMA((8, NZ)),
            DMA((8, NZ)),
            DMA((NY, NZ)),
            DMA((NY, NZ)),
            DMA((NZ,)),
            DMA((NZ,)),
        ],
        asks, keys, queries, d_aug, out_proj, mixed_t, total, tile_weight,
        in_specs=[S] + [V] * 7,
    )
    return (loss[0], query_grad, knowledge_grad, label_step)


def solution(mesh):
    placed = (
        P(("dp", "table"), None),
        P(("dp", "table"), None),
        P("table", None, None),
        P(),
        P("table", None, None),
        P(("dp", "table"), None),
        P(("dp", "table"), None),
    )
    return jax.shard_map(
        on_device,
        mesh=mesh,
        in_specs=placed,
        out_specs=(
            P(("dp", "table")),
            P(("dp", "table"), None),
            P("table", "dp", None),
            P("table", "dp", None),
        ),
        check_vma=False,
    )
```

```python
import functools
import math

import jax
import jax.numpy as jnp
from jax import lax
from jax.experimental import pallas as pl
from jax.experimental.pallas import tpu as pltpu
from jax.sharding import PartitionSpec as P

MESH = pl.DeviceIdType.MESH
DMA = pltpu.SemaphoreType.DMA
F32 = jnp.float32
BF16 = jnp.bfloat16
HEADS = 12
PAIRS = 6
Q = 128
D = 768
NZ = 8
NX = 4
NY = 4
epsilon = 1e-06
LOG2E = 1.4426950408889634
VMEM_LIMIT = 50 << 20


def where_am_i():
    dp, t = lax.axis_index("dp"), lax.axis_index("table")
    return dp // 2, dp % 2, t // NX, t % NX


def dev(y, c, z, x):
    return (y * 2 + c, z * NX + x)


def greet(peers):
    barrier = pltpu.get_barrier_semaphore()
    for peer in peers:
        pl.semaphore_signal(barrier, inc=1, device_id=peer, device_id_type=MESH)
    pl.semaphore_wait(barrier, len(peers))


def remote(src, dst, send, recv, to):
    return pltpu.make_async_remote_copy(
        src_ref=src, dst_ref=dst, send_sem=send, recv_sem=recv, device_id=to, device_id_type=MESH
    )


def nt(a, b):
    return lax.dot_general(a, b, (((1,), (1,)), ((), ())), preferred_element_type=F32)


def tn(a, b):
    return lax.dot_general(a, b, (((0,), (0,)), ((), ())), preferred_element_type=F32)


def nn(a, b):
    return jnp.dot(a, b, preferred_element_type=F32)


def stack_heads(rows, stacked_ref):
    lane = lax.broadcasted_iota(jnp.int32, (Q, 128), 1)
    for p in range(PAIRS):
        part = rows[:, p * 128 : (p + 1) * 128]
        stacked_ref[p, :Q] = jnp.where(lane < 64, part, jnp.zeros_like(part))
        stacked_ref[p, Q:] = jnp.where(lane < 64, jnp.zeros_like(part), part)


def unstack_heads(both):
    return jnp.concatenate([both[0:64, 0:Q], both[64:128, Q : 2 * Q]], axis=0)


def weight_block(tw):
    tw2 = jnp.concatenate([tw, tw], axis=1)
    return jnp.broadcast_to(tw2[:, None, :], (NX, 64, 2 * Q)).reshape(NX * 64, 2 * Q)


XC = [(dx, dc) for dx in range(NX) for dc in range(2)]


def keys_kernel(
    know, wanted, queries, tile_weight, out_proj, msg,
    keys, aug, mixed_t, total, asks, ints,
    half, r0, r1, r2, l0, l1, l2, far, stage, stacked, acc, mid,
    ask_smem, z_send, z_recv, x_send, x_recv, a_send, a_recv, m_send, m_recv, n_send, n_recv, l_sem,
):
    y, c, z, x = where_am_i()
    me = x * 2 + c
    right, left = dev(y, c, (z + 1) % NZ, x), dev(y, c, (z + NZ - 1) % NZ, x)
    group = [((x + dx) % NX, (c + dc) % 2) for dx, dc in XC]
    greet(
        [dev(y, pc, z, px) for px, pc in group[1:]]
        + [dev(y, c, (z + d) % NZ, x) for d in range(1, NZ)]
    )
    half[...] = know[:, pl.ds(pl.multiple_of(c * 32, 32), 32), :]
    ask_copies = []
    for j in range(1, 8):
        px, pc = group[j]
        cp = remote(wanted, asks.at[me], a_send.at[j], a_recv.at[j], dev(y, pc, z, px))
        cp.start()
        ask_copies.append(cp)
    ring = {}
    slots = ((half, r0, r1, r2, far), (half, l0, l1, l2, far))

    def ring_send(way, step, k):
        piece = pl.ds(k * 2, 2)
        cp = remote(
            slots[way][step].at[piece], slots[way][step + 1].at[piece],
            z_send.at[way, step, k], z_recv.at[way, step, k], right if way == 0 else left,
        )
        cp.start()
        ring[way, step, k] = cp

    for k in range(4):
        for way in (0, 1):
            ring_send(way, 0, k)
    m_copies = []
    for dx in range(1, NX):
        px = (x + dx) % NX
        cp = remote(msg.at[px], mid.at[x], m_send.at[dx], m_recv.at[dx], dev(y, c, z, px))
        cp.start()
        m_copies.append(cp)
    asks[me] = wanted[...]
    mid[x] = msg[x]
    stack_heads(queries[...], stacked)
    acc[...] = jnp.zeros_like(acc)
    total[...] = jnp.zeros_like(total)
    for cp in ask_copies:
        cp.wait()
    cp = pltpu.make_async_copy(asks, ask_smem, l_sem)
    cp.start()
    cp.wait()
    sent = []

    def serve(zo, shard):
        row = pl.ds(pl.multiple_of(c * 32, 32), 32)
        for j, (px, pc) in enumerate(group):
            tile = ask_smem[px * 2 + pc, zo, x]
            if j == 0:
                keys[zo * NX + x, row] = shard[tile]
                continue
            stage[j, zo] = shard[tile]
            cp = remote(
                stage.at[j, zo], keys.at[zo * NX + x, row], x_send.at[j, zo], x_recv.at[j, zo],
                dev(y, pc, z, px),
            )
            cp.start()
            sent.append(cp)

    def arrived(zo):
        for j in range(1, 8):
            row = pl.ds(0, 32)
            remote(
                stage.at[j, zo], keys.at[zo * NX, row], x_send.at[j, zo], x_recv.at[j, zo], right
            ).wait_recv()

    def attend(zo):
        w = weight_block(tile_weight[zo])

        def pair(p, carry):
            lanes = pl.ds(pl.multiple_of(p * 128, 128), 128)
            k = keys[pl.ds(zo * NX, NX), :, lanes].reshape(256, 128)
            capped = jnp.tanh(nt(k, stacked[p]) * (1.0 / 80.0))
            raw = w * jnp.exp2(capped * (10.0 * LOG2E))
            total[p] = total[p] + jnp.sum(raw, axis=0, keepdims=True)
            acc[p] = acc[p] + tn(k, raw.astype(BF16))
            return carry

        lax.fori_loop(0, PAIRS, pair, 0)

    def wait_step(way, step, k):
        ring[way, step, k].wait_recv()

    serve(z, half)
    for cp in m_copies:
        cp.wait()
    n_copies = []
    for d in range(1, NZ):
        zp = (z + d) % NZ
        cp = remote(
            mid.at[:, zp], ints.at[z], n_send.at[d], n_recv.at[d], dev(y, c, zp, x)
        )
        cp.start()
        n_copies.append(cp)
    ints[z] = mid[:, z]
    pending = [z]
    for step in range(1, 4):
        for k in range(4):
            for way in (0, 1):
                wait_step(way, step - 1, k)
                if step < 3 or (k < 2) == (way == 0):
                    ring_send(way, step, k)
        serve((z + NZ - step) % NZ, slots[0][step])
        serve((z + step) % NZ, slots[1][step])
        for zo in pending:
            arrived(zo)
            attend(zo)
        pending = [(z + NZ - step) % NZ, (z + step) % NZ]
    for k in range(4):
        wait_step(0 if k < 2 else 1, 3, k)
    serve((z + 4) % NZ, far)
    for zo in pending:
        arrived(zo)
        attend(zo)
    for cp in n_copies:
        cp.wait()
    arrived((z + 4) % NZ)
    attend((z + 4) % NZ)
    for p in range(PAIRS):
        mixed_t[p] = unstack_heads(acc[p] / total[p])
    mixed = jnp.concatenate([mixed_t[p].T for p in range(PAIRS)], axis=1).astype(BF16)
    aug[...] = (queries[...].astype(F32) + nn(mixed, out_proj[...])).astype(BF16)
    for cp in ring.values():
        cp.wait_send()
    for cp in sent:
        cp.wait_send()


def labels_kernel(
    aug, ints, wcol, labels,
    d_aug, loss, label_step,
    rows, served, got, back, back_got, lstage, lgot, dlogit, onehot, lpart, lsend, lrecv,
    psend, prbuf, label_grad, label_got,
    z_send, z_recv, x_send, x_recv, b_send, b_recv, s_send, s_recv, p_send, p_recv, q_send, q_recv,
    g_send, g_recv,
):
    y, c, z, x = where_am_i()
    dp = y * 2 + c
    right, left = dev(y, c, (z + 1) % NZ, x), dev(y, c, (z + NZ - 1) % NZ, x)
    greet(
        [dev(y, c, z, (x + dx) % NX) for dx in range(1, NX)]
        + [dev(y, c, (z + d) % NZ, x) for d in range(1, NZ)]
        + [((dp + d) % 8, z * NX + x) for d in range(1, 8)]
    )
    ring = {}

    def ring_send(way, step, k):
        own = (z + NZ - step) % NZ if way == 0 else (z + step) % NZ
        piece = pl.ds(k * 32, 32)
        src = aug.at[piece] if step == 0 else rows.at[own, piece]
        cp = remote(
            src, rows.at[own, piece], z_send.at[way, step, k], z_recv.at[way, step, k],
            right if way == 0 else left,
        )
        cp.start()
        ring[way, step, k] = cp

    for k in range(4):
        for way in (0, 1):
            ring_send(way, 0, k)
    rows[z] = aug[...]
    query = lax.broadcasted_iota(jnp.int32, (Q, 128), 0)

    def hot(i, carry):
        onehot[i] = jnp.where(query == ints[i, x, 5:6, :], 1.0, 0.0).astype(BF16)
        return carry

    lax.fori_loop(0, NZ, hot, 0)
    sent = []

    def serve(zs):
        picked = tn(onehot[zs], rows[zs]).astype(BF16)
        served[zs] = picked.reshape(NX, 2, 16, D)
        got[zs, :, x] = served[zs, x]
        for dx in range(1, NX):
            px = (x + dx) % NX
            cp = remote(
                served.at[zs, px], got.at[zs, :, x], x_send.at[dx, zs], x_recv.at[dx, zs],
                dev(y, c, z, px),
            )
            cp.start()
            sent.append(cp)

    label = lax.broadcasted_iota(jnp.int32, (64, 512), 1)
    lane = lax.broadcasted_iota(jnp.int32, (NX, 16, 128), 2)
    lstage[...] = jnp.zeros_like(lstage)

    def work(zs):
        for dx in range(1, NX):
            remote(
                served.at[0, 0], got.at[zs, :, 0], x_send.at[dx, zs], x_recv.at[dx, zs], right
            ).wait_recv()

        def cluster(cl, carry):
            entries = got[zs, cl].reshape(64, D)
            logits = nt(entries, labels[cl])
            want = wcol[zs * 2 + cl]
            live = (want[:, 4:5] > 0).astype(F32)
            hit = label == want[:, 0:1]
            for j in range(1, 4):
                hit = hit | (label == want[:, j : j + 1])
            e = jnp.exp(-jnp.abs(logits))
            soft = jnp.maximum(logits, 0.0) + jnp.log1p(e)
            pair_loss = jnp.sum(soft - jnp.where(hit, logits, 0.0), axis=1, keepdims=True) * live
            inv = 1.0 / (1.0 + e)
            sig = jnp.where(logits >= 0, inv, 1.0 - inv)
            dl = ((sig - jnp.where(hit, 1.0, 0.0)) * live).astype(BF16)
            dlogit[zs, cl] = dl
            back[zs, cl] = nn(dl, labels[cl]).astype(BF16).reshape(NX, 16, D)
            spread = jnp.broadcast_to(pair_loss, (64, 128)).reshape(NX, 16, 128)
            lstage[:, cl] = jnp.where(lane == zs, spread, lstage[:, cl])
            return carry

        lax.fori_loop(0, 2, cluster, 0)

    def send_back(zs):
        back_got[zs, x] = back[zs, :, x]
        for dx in range(1, NX):
            px = (x + dx) % NX
            cp = remote(
                back.at[zs, :, px], back_got.at[zs, x], b_send.at[dx, zs], b_recv.at[dx, zs],
                dev(y, c, z, px),
            )
            cp.start()
            sent.append(cp)

    serve(z)
    pending = [z]
    for step in range(1, 4):
        for k in range(4):
            for way in (0, 1):
                ring[way, step - 1, k].wait_recv()
                if step < 3 or (k < 2) == (way == 0):
                    ring_send(way, step, k)
        fresh = [(z + NZ - step) % NZ, (z + step) % NZ]
        for zs in fresh:
            serve(zs)
        for zs in pending:
            work(zs)
        pending = fresh
    for k in range(4):
        ring[0 if k < 2 else 1, 3, k].wait_recv()
    serve((z + 4) % NZ)
    for zs in pending:
        work(zs)
        send_back(zs)
    work((z + 4) % NZ)
    for d in (4, 2, 6, 1, 7, 0):
        send_back((z + d) % NZ)
    loss_copies = []
    for dx in range(1, NX):
        px = (x + dx) % NX
        cp = remote(lstage.at[px], lgot.at[x], s_send.at[dx], s_recv.at[dx], dev(y, c, z, px))
        cp.start()
        loss_copies.append(cp)
    lgot[x] = lstage[x]

    def partial(zs):
        for dx in range(1, NX):
            remote(
                back.at[0, :, 0], back_got.at[zs, 0], b_send.at[dx, zs], b_recv.at[dx, zs], right
            ).wait_recv()
        return nn(onehot[zs], back_got[zs].reshape(128, D))

    label_copies = []

    def label_part(cl):
        entries = got[:, cl].reshape(512, D)
        for part in range(2):
            columns = slice(part * 256, part * 256 + 256)
            value = tn(dlogit[:, cl, :, columns].reshape(512, 256), entries)
            label_grad[cl, part * 4 : part * 4 + 4] = value.astype(BF16).reshape(4, 64, D)
        label_got[cl, dp] = label_grad[cl, dp]
        for d in range(1, 8):
            to = (dp + d) % 8
            cp = remote(
                label_grad.at[cl, to], label_got.at[cl, dp], g_send.at[cl, d], g_recv.at[cl, d],
                (to, z * NX + x),
            )
            cp.start()
            label_copies.append(cp)

    p_copies = {}

    def chain_send(way, step, h, value):
        piece = pl.ds(h * 64, 64)
        psend[way, step, piece] = value.astype(BF16)
        cp = remote(
            psend.at[way, step, piece], prbuf.at[way, step, piece],
            p_send.at[way, step, h], p_recv.at[way, step, h], right if way == 0 else left,
        )
        cp.start()
        p_copies[way, step, h] = cp

    label_part(0)
    far = partial((z + 4) % NZ)
    for way in (0, 1):
        chain_send(way, 0, way, far[way * 64 : way * 64 + 64])
    label_part(1)
    for step in range(1, 4):
        d = 4 - step
        own = [partial((z + d) % NZ), partial((z + NZ - d) % NZ)]
        for h in (0, 1):
            for way in (h, 1 - h):
                value = own[way][h * 64 : h * 64 + 64]
                if (way, step - 1, h) in p_copies:
                    p_copies[way, step - 1, h].wait_recv()
                    value = value + prbuf[way, step - 1, h * 64 : h * 64 + 64].astype(F32)
                chain_send(way, step, h, value)
    mine = partial(z)
    for cp in loss_copies:
        cp.wait()
    losses = jnp.concatenate([lgot[i].reshape(32, 128) for i in range(NX)], axis=0).astype(BF16)
    out_lane = lax.broadcasted_iota(jnp.int32, (Q, 128), 1)
    lpart[...] = jnp.zeros_like(lpart)

    def loss_of(i, carry):
        lpart[...] = lpart[...] + jnp.where(out_lane == i, nn(onehot[i], losses), 0.0)
        return carry

    lax.fori_loop(0, NZ, loss_of, 0)
    lsend[...] = lpart[...].T[:NZ]
    l_copies = []
    for d in range(1, NZ):
        zp = (z + d) % NZ
        cp = remote(lsend, lrecv.at[z], q_send.at[d], q_recv.at[d], dev(y, c, zp, x))
        cp.start()
        l_copies.append(cp)
    lrecv[z] = lsend[...]
    for h in (0, 1):
        for way in (0, 1):
            p_copies[way, 3, h].wait_recv()
    d_aug[...] = mine + prbuf[0, 3].astype(F32) + prbuf[1, 3].astype(F32)
    for cp in l_copies:
        cp.wait()
    loss[...] = jnp.sum(lrecv[:, pl.ds(z, 1), :], axis=0) * (1.0 / 2048.0)
    for cp in label_copies:
        cp.wait()
    for cl in range(2):
        grad = label_got[cl, 0].astype(F32)
        for i in range(1, 8):
            grad = grad + label_got[cl, i].astype(F32)
        square = jnp.mean(grad * grad, axis=1, keepdims=True)
        label_step[cl] = grad * lax.rsqrt(square + epsilon)
    for cp in p_copies.values():
        cp.wait_send()
    for cp in ring.values():
        cp.wait_send()
    for cp in sent:
        cp.wait_send()


def grads_kernel(
    asks, keys, queries, d_aug, out_proj, mixed_t, total, tile_weight,
    query_grad, know_grad,
    stacked, d_acc, delta, gsend, ggot, ysend, ygot, zsend, zgot,
    x_send, x_recv, y_send, y_recv, z_send, z_recv,
):
    y, c, z, x = where_am_i()
    me = x * 2 + c
    group = [((x + dx) % NX, (c + dc) % 2) for dx, dc in XC]
    greet(
        [dev(y, pc, z, px) for px, pc in group[1:]]
        + [dev((y + d) % NY, c, z, x) for d in range(1, NY)]
        + [dev(y, c, (z + d) % NZ, x) for d in range(1, NZ)]
    )
    d_rows = d_aug[...]
    back_proj = nt(d_rows.astype(BF16), out_proj[...]).astype(BF16)
    stack_heads(queries[...], stacked.at[:, 0:256])
    stack_heads(back_proj, stacked.at[:, 256:512])
    for p in range(PAIRS):
        product = mixed_t[p] * back_proj[:, p * 128 : (p + 1) * 128].astype(F32).T
        delta[p] = jnp.concatenate(
            [
                jnp.sum(product[:64], axis=0, keepdims=True),
                jnp.sum(product[64:], axis=0, keepdims=True),
            ],
            axis=1,
        )
    d_acc[...] = jnp.zeros_like(d_acc)

    def compute(zo):
        w = weight_block(tile_weight[zo])

        def pair(p, carry):
            lanes = pl.ds(pl.multiple_of(p * 128, 128), 128)
            k = keys[pl.ds(zo * NX, NX), :, lanes].reshape(256, 128)
            rows = stacked[p]
            products = nt(k, rows)
            capped = jnp.tanh(products[:, :256] * (1.0 / 80.0))
            soft = w * jnp.exp2(capped * (10.0 * LOG2E)) * (1.0 / total[p])
            d_score = soft * (products[:, 256:] - delta[p]) * ((1.0 - capped * capped) * 0.125)
            both = jnp.concatenate([d_score.astype(BF16), soft.astype(BF16)], axis=1)
            d_acc[p] = d_acc[p] + tn(k, both[:, :256])
            grad = nn(both, rows).reshape(NX, NY, 2, 8, 128)
            for side in range(2):
                gsend[zo, :, side, :, lanes] = grad[:, :, side].reshape(NX, 32, 128).astype(BF16)
            return carry

        lax.fori_loop(0, PAIRS, pair, 0)
        ggot[me, zo] = gsend[zo, x, c]
        for j in range(1, 8):
            px, pc = group[j]
            remote(
                gsend.at[zo, px, pc], ggot.at[me, zo], x_send.at[j, zo], x_recv.at[j, zo],
                dev(y, pc, z, px),
            ).start()

    def gather_tiles(zo):
        for j in range(1, 8):
            remote(
                gsend.at[zo, 0, 0], ggot.at[0, zo], x_send.at[j, zo], x_recv.at[j, zo],
                dev(y, c, z, x),
            ).wait_recv()
        tiles = [asks[s, zo, x] for s in range(8)]

        def two_tiles(k2, carry):
            sums = []
            for k in range(2):
                value = jnp.zeros((32, D), F32)
                for s in range(8):
                    value = value + ggot[s, zo].astype(F32) * jnp.where(
                        tiles[s] == k2 * 2 + k, 1.0, 0.0
                    )
                sums.append(value.reshape(NY, 1, 8, D))
            joined = jnp.concatenate(sums, axis=1).reshape(NY, 16, D).astype(BF16)
            ysend[zo, :, k2] = joined
            return carry

        lax.fori_loop(0, 4, two_tiles, 0)
        ygot[y, zo] = ysend[zo, y]
        for d in range(1, NY):
            py = (y + d) % NY
            remote(
                ysend.at[zo, py], ygot.at[y, zo], y_send.at[d, zo], y_recv.at[d, zo],
                dev(py, c, z, x),
            ).start()

    def gather_shards(zo, own):
        for d in range(1, NY):
            remote(
                ysend.at[zo, 0], ygot.at[0, zo], y_send.at[d, zo], y_recv.at[d, zo],
                dev(y, c, z, x),
            ).wait_recv()
        value = ygot[0, zo].astype(F32)
        for i in range(1, NY):
            value = value + ygot[i, zo].astype(F32)
        zsend[zo] = value.astype(BF16)

        @pl.when(own == 0)
        def _():
            zgot[z] = zsend[z]

        @pl.when(own != 0)
        def _():
            remote(
                zsend.at[zo], zgot.at[z], z_send.at[own], z_recv.at[own], dev(y, c, zo, x)
            ).start()

    def offset(i):
        return (3 * (i + 1)) % NZ

    def body(i, carry):
        @pl.when(i < 8)
        def _():
            compute((z + offset(i)) % NZ)

        @pl.when((i >= 3) & (i < 11))
        def _():
            gather_tiles((z + offset(i - 3)) % NZ)

        @pl.when(i >= 5)
        def _():
            gather_shards((z + offset(i - 5)) % NZ, offset(i - 5))

        return carry

    lax.fori_loop(0, 13, body, 0)
    d_query = jnp.concatenate([unstack_heads(d_acc[p]).T for p in range(PAIRS)], axis=1)
    query_grad[...] = d_rows + d_query
    for d in range(1, NZ):
        remote(zsend.at[0], zgot.at[0], z_send.at[d], z_recv.at[d], dev(y, c, z, x)).wait_recv()
    value = zgot[0].astype(F32)
    for i in range(1, NZ):
        value = value + zgot[i].astype(F32)
    know_grad[...] = value.reshape(8, 8, D)

    def drain(zo, carry):
        for j in range(1, 8):
            remote(
                gsend.at[zo, 0, 0], ggot.at[0, zo], x_send.at[j, zo], x_recv.at[j, zo],
                dev(y, c, z, x),
            ).wait_send()
        for d in range(1, NY):
            remote(
                ysend.at[zo, 0], ygot.at[0, zo], y_send.at[d, zo], y_recv.at[d, zo],
                dev(y, c, z, x),
            ).wait_send()
        return carry

    lax.fori_loop(0, NZ, drain, 0)
    for d in range(1, NZ):
        remote(zsend.at[0], zgot.at[0], z_send.at[d], z_recv.at[d], dev(y, c, z, x)).wait_send()


V = pl.BlockSpec(memory_space=pltpu.VMEM)
S = pl.BlockSpec(memory_space=pltpu.SMEM)


def run(kernel, number, outs, scratch, *args, in_specs=None):
    return pl.pallas_call(
        kernel,
        out_shape=[jax.ShapeDtypeStruct(shape, dtype) for shape, dtype in outs],
        in_specs=in_specs or [V] * len(args),
        out_specs=[V] * len(outs),
        scratch_shapes=scratch,
        compiler_params=pltpu.CompilerParams(
            collective_id=number, has_side_effects=True, vmem_limit_bytes=VMEM_LIMIT
        ),
        cost_estimate=pl.CostEstimate(
            flops=4_000_000_000, bytes_accessed=40_000_000, transcendentals=6_000_000
        ),
    )(*args)


def prepare(tile_ids, cluster_ids, positive_picks):
    tiles, ids, picks = tile_ids.T, cluster_ids.T, positive_picks.T
    owner = jnp.arange(32, dtype=jnp.int32)
    hits = (tiles // 8)[:, None, :] == owner[None, :, None]
    tile_weight = jnp.sum(hits.astype(F32), axis=0)
    wanted = jnp.max(jnp.where(hits, (tiles % 8)[:, None, :], 0), axis=(0, 2))
    wanted = jnp.pad(wanted.reshape(NZ, NX), ((0, 0), (0, 128 - NX)))
    cluster = jnp.arange(64, dtype=jnp.int32)
    member = jnp.any(ids[:, None, :] == cluster[None, :, None], axis=0)
    before = (jnp.arange(Q)[:, None] < jnp.arange(Q)[None, :]).astype(BF16)
    rank = jnp.dot(member.astype(BF16), before, preferred_element_type=F32).astype(jnp.int32)
    rank = jnp.where(member, rank, -1)
    slot = jnp.arange(16, dtype=jnp.int32)
    held = rank[:, None, :] == slot[None, :, None]
    query = jnp.arange(Q, dtype=jnp.int32)
    slot_query = Q + jnp.sum(jnp.where(held, query - Q, 0), axis=2)
    live = (slot_query < Q).astype(jnp.int32)
    column = picks // 512
    pick_cluster = jnp.sum(
        jnp.where(column[:, None, :] == jnp.arange(4)[None, :, None], ids[None], 0), axis=1
    )
    pick_label = picks % 512 + 1
    wanted_label = [
        jnp.sum(
            jnp.where(
                held & (pick_cluster[j][None, None, :] == cluster[:, None, None]),
                pick_label[j],
                0,
            ),
            axis=2,
        )
        - 1
        for j in range(4)
    ]
    parts = [a.reshape(NZ, NX, 1, 32) for a in wanted_label + [live]]
    parts = jnp.pad(jnp.concatenate(parts, axis=2), ((0, 0), (0, 0), (0, 0), (0, 96)))
    slots = jnp.broadcast_to(slot_query.reshape(NZ, 1, 1, 128), (NZ, NX, 1, 128))
    msg = jnp.concatenate([parts, slots, jnp.zeros((NZ, NX, 2, 128), jnp.int32)], axis=2)
    return tile_weight.reshape(NZ, NX, Q), wanted, msg.transpose(1, 0, 2, 3)


def on_device(queries, tile_ids, knowledge, out_proj, labels, cluster_ids, positive_picks):
    tile_weight, wanted, msg = prepare(tile_ids, cluster_ids, positive_picks)
    keys, aug, mixed_t, total, asks, ints = run(
        keys_kernel,
        1,
        [
            ((32, 64, D), BF16),
            ((Q, D), BF16),
            ((PAIRS, 128, Q), F32),
            ((PAIRS, 1, 2 * Q), F32),
            ((8, 8, 128), jnp.int32),
            ((NZ, NX, 8, 128), jnp.int32),
        ],
        [
            *[pltpu.VMEM((8, 32, D), BF16) for _ in range(8)],
            pltpu.VMEM((8, NZ, 32, D), BF16),
            pltpu.VMEM((PAIRS, 2 * Q, 128), BF16),
            pltpu.VMEM((PAIRS, 128, 2 * Q), F32),
            pltpu.VMEM((NX, NZ, 8, 128), jnp.int32),
            pltpu.SMEM((8, 8, 128), jnp.int32),
            DMA((2, 4, 4)),
            DMA((2, 4, 4)),
            DMA((8, NZ)),
            DMA((8, NZ)),
            DMA((8,)),
            DMA((8,)),
            DMA((NX,)),
            DMA((NX,)),
            DMA((NZ,)),
            DMA((NZ,)),
            DMA,
        ],
        knowledge, wanted, queries, tile_weight, out_proj, msg,
    )
    wcol = ints[:, :, :5, :32].reshape(NZ, NX, 5, 2, 16).transpose(0, 3, 1, 4, 2)
    wcol = jnp.pad(wcol.reshape(16, 64, 5), ((0, 0), (0, 0), (0, 3)))
    d_aug, loss, label_step = run(
        labels_kernel,
        2,
        [((Q, D), F32), ((1, Q), F32), ((2, 64, D), F32)],
        [
            pltpu.VMEM((NZ, Q, D), BF16),
            pltpu.VMEM((NZ, NX, 2, 16, D), BF16),
            pltpu.VMEM((NZ, 2, NX, 16, D), BF16),
            pltpu.VMEM((NZ, 2, NX, 16, D), BF16),
            pltpu.VMEM((NZ, NX, 2, 16, D), BF16),
            pltpu.VMEM((NX, 2, 16, 128), F32),
            pltpu.VMEM((NX, 2, 16, 128), F32),
            pltpu.VMEM((NZ, 2, 64, 512), BF16),
            pltpu.VMEM((NZ, Q, 128), BF16),
            pltpu.VMEM((Q, 128), F32),
            pltpu.VMEM((NZ, 128), F32),
            pltpu.VMEM((NZ, NZ, 128), F32),
            pltpu.VMEM((2, 4, Q, D), BF16),
            pltpu.VMEM((2, 4, Q, D), BF16),
            pltpu.VMEM((2, 8, 64, D), BF16),
            pltpu.VMEM((2, 8, 64, D), BF16),
            DMA((2, 4, 4)),
            DMA((2, 4, 4)),
            DMA((NX, NZ)),
            DMA((NX, NZ)),
            DMA((NX, NZ)),
            DMA((NX, NZ)),
            DMA((NX,)),
            DMA((NX,)),
            DMA((2, 4, 2)),
            DMA((2, 4, 2)),
            DMA((NZ,)),
            DMA((NZ,)),
            DMA((2, 8)),
            DMA((2, 8)),
        ],
        aug, ints, wcol, labels,
    )
    query_grad, knowledge_grad = run(
        grads_kernel,
        3,
        [((Q, D), F32), ((8, 8, D), F32)],
        [
            pltpu.VMEM((PAIRS, 4 * Q, 128), BF16),
            pltpu.VMEM((PAIRS, 128, 2 * Q), F32),
            pltpu.VMEM((PAIRS, 1, 2 * Q), F32),
            pltpu.VMEM((NZ, NX, 2, 32, D), BF16),
            pltpu.VMEM((8, NZ, 32, D), BF16),
            pltpu.VMEM((NZ, NY, 4, 16, D), BF16),
            pltpu.VMEM((NY, NZ, 4, 16, D), BF16),
            pltpu.VMEM((NZ, 4, 16, D), BF16),
            pltpu.VMEM((NZ, 4, 16, D), BF16),
            DMA((8, NZ)),
            DMA((8, NZ)),
            DMA((NY, NZ)),
            DMA((NY, NZ)),
            DMA((NZ,)),
            DMA((NZ,)),
        ],
        asks, keys, queries, d_aug, out_proj, mixed_t, total, tile_weight,
        in_specs=[S] + [V] * 7,
    )
    return (loss[0], query_grad, knowledge_grad, label_step)


def solution(mesh):
    placed = (
        P(("dp", "table"), None),
        P(("dp", "table"), None),
        P("table", None, None),
        P(),
        P("table", None, None),
        P(("dp", "table"), None),
        P(("dp", "table"), None),
    )
    return jax.shard_map(
        on_device,
        mesh=mesh,
        in_specs=placed,
        out_specs=(
            P(("dp", "table")),
            P(("dp", "table"), None),
            P("table", "dp", None),
            P("table", "dp", None),
        ),
        check_vma=False,
    )
```

```python
import jax
import jax.numpy as jnp
from jax import lax
from jax.experimental import pallas as pl
from jax.experimental.pallas import tpu as pltpu
from jax.sharding import PartitionSpec as P

MESH = pl.DeviceIdType.MESH
DMA = pltpu.SemaphoreType.DMA
F32 = jnp.float32
BF16 = jnp.bfloat16
PAIRS = 6
Q = 128
D = 768
NZ = 8
NX = 4
NY = 4
epsilon = 1e-06
LOG2E = 1.4426950408889634
VMEM_LIMIT = 56 << 20


def where_am_i():
    dp, t = lax.axis_index("dp"), lax.axis_index("table")
    return dp // 2, dp % 2, t // NX, t % NX


def dev(y, c, z, x):
    return (y * 2 + c, z * NX + x)


def greet(peers):
    barrier = pltpu.get_barrier_semaphore()
    for peer in peers:
        pl.semaphore_signal(barrier, inc=1, device_id=peer, device_id_type=MESH)
    pl.semaphore_wait(barrier, len(peers))


def remote(src, dst, send, recv, to):
    return pltpu.make_async_remote_copy(
        src_ref=src, dst_ref=dst, send_sem=send, recv_sem=recv, device_id=to, device_id_type=MESH
    )


def nt(a, b):
    return lax.dot_general(a, b, (((1,), (1,)), ((), ())), preferred_element_type=F32)


def tn(a, b):
    return lax.dot_general(a, b, (((0,), (0,)), ((), ())), preferred_element_type=F32)


def nn(a, b):
    return jnp.dot(a, b, preferred_element_type=F32)


def stack_heads(rows, stacked_ref):
    lane = lax.broadcasted_iota(jnp.int32, (Q, 128), 1)
    for p in range(PAIRS):
        part = rows[:, p * 128 : (p + 1) * 128]
        stacked_ref[p, :Q] = jnp.where(lane < 64, part, jnp.zeros_like(part))
        stacked_ref[p, Q:] = jnp.where(lane < 64, jnp.zeros_like(part), part)


def unstack_heads(both):
    return jnp.concatenate([both[0:64, 0:Q], both[64:128, Q : 2 * Q]], axis=0)


def weight_block(tw):
    tw2 = jnp.concatenate([tw, tw], axis=1)
    return jnp.broadcast_to(tw2[:, None, :], (NX, 64, 2 * Q)).reshape(NX * 64, 2 * Q)


XC = [(dx, dc) for dx in range(NX) for dc in range(2)]


def keys_kernel(
    know, numbers, queries, out_proj,
    keys, aug, mixed_t, total, tile_weight, onehot, facts, ask_smem,
    wanted, asks, half, r0, r1, r2, l0, l1, l2, far, stage, stacked, acc, note, noted, fact,
    z_send, z_recv, x_send, x_recv, a_send, a_recv, m_send, m_recv, n_send, n_recv, l_sem,
):
    y, c, z, x = where_am_i()
    dp = y * 2 + c
    me = x * 2 + c
    right, left = dev(y, c, (z + 1) % NZ, x), dev(y, c, (z + NZ - 1) % NZ, x)
    group = [((x + dx) % NX, (c + dc) % 2) for dx, dc in XC]
    greet(
        [dev(y, pc, z, px) for px, pc in group[1:]]
        + [dev(y, c, (z + d) % NZ, x) for d in range(1, NZ)]
        + [((dp + d) % 8, z * NX + x) for d in range(1, 8)]
    )
    half[...] = know[:, pl.ds(pl.multiple_of(c * 32, 32), 32), :]
    ring = {}
    slots = ((half, r0, r1, r2, far), (half, l0, l1, l2, far))

    def ring_send(way, step, k):
        piece = pl.ds(k * 2, 2)
        cp = remote(
            slots[way][step].at[piece], slots[way][step + 1].at[piece],
            z_send.at[way, step, k], z_recv.at[way, step, k], right if way == 0 else left,
        )
        cp.start()
        ring[way, step, k] = cp

    for k in range(4):
        for way in (0, 1):
            ring_send(way, 0, k)
    owner = lax.broadcasted_iota(jnp.int32, (32, Q), 0)
    weight, tile = jnp.zeros((32, Q), F32), jnp.zeros((32, Q), jnp.int32)
    for r in range(4):
        named = numbers[r : r + 1, :]
        hit = (named >> 3) == owner
        weight = weight + jnp.where(hit, 1.0, 0.0)
        tile = jnp.maximum(tile, jnp.where(hit, named & 7, 0))
    wanted[...] = jnp.broadcast_to(jnp.max(tile, axis=1, keepdims=True), (32, 128))
    ask_copies = []
    for j in range(1, 8):
        px, pc = group[j]
        cp = remote(wanted, asks.at[me], a_send.at[j], a_recv.at[j], dev(y, pc, z, px))
        cp.start()
        ask_copies.append(cp)
    asks[me] = wanted[...]
    for zo in range(NZ):
        tile_weight[zo, 0:NX] = weight[zo * NX : zo * NX + NX]
    cluster = lax.broadcasted_iota(jnp.int32, (64, Q), 0)
    ids = [numbers[4 + i : 5 + i, :] for i in range(4)]
    member = ids[0] == cluster
    for i in range(1, 4):
        member = member | (ids[i] == cluster)
    row = lax.broadcasted_iota(jnp.int32, (Q, 128), 0)
    lane = lax.broadcasted_iota(jnp.int32, (Q, 128), 1)
    before = jnp.where(row < lane, 1.0, 0.0).astype(BF16)
    rank = nn(jnp.where(member, 1.0, 0.0).astype(BF16), before)
    rank = jnp.where(member, rank, -1.0)
    picks = [numbers[8 + j : 9 + j, :] for j in range(4)]
    columns = []
    for j in range(4):
        column = picks[j] >> 9
        named = jnp.where(column == 0, ids[0], 0)
        for i in range(1, 4):
            named = jnp.where(column == i, ids[i], named)
        columns.append(named)
    columns += [(pick & 511) >> 8 for pick in picks] + [pick & 255 for pick in picks]
    columns += [jnp.ones_like(picks[0])] + [jnp.zeros_like(picks[0])] * 3
    columns = jnp.concatenate(columns, axis=0).astype(F32)
    for i in range(NZ):
        note[i, 0:8] = rank[i * 8 : i * 8 + 8]
        note[i, 8:24] = columns
    note_copies = []
    for d in range(1, NZ):
        zp = (z + d) % NZ
        cp = remote(
            note.at[zp], noted.at[NZ - d], m_send.at[d], m_recv.at[NZ - d], dev(y, c, zp, x)
        )
        cp.start()
        note_copies.append(cp)
    noted[0] = note[z]

    def slots_and_facts():
        for d in range(1, NZ):
            remote(note.at[0], noted.at[d], m_send.at[d], m_recv.at[d], right).wait_recv()
        spread = jnp.where(
            lax.broadcasted_iota(jnp.int32, (16, 128), 0)
            == lax.broadcasted_iota(jnp.int32, (16, 128), 1) // 16,
            1.0, 0.0,
        ).astype(BF16)
        place = (lane % 16).astype(F32)
        about = noted[:, 8:24, :].reshape(128, Q).T
        value = jnp.zeros((128, 128), F32)
        for o in range(NZ):
            hot = jnp.where(tn(noted[o, 0:16].astype(BF16), spread) == place, 1.0, 0.0).astype(BF16)
            onehot[o] = hot
            value = value + tn(hot, jnp.where(lane // 16 == o, about, 0.0).astype(BF16))
        fact[...] = value.reshape(NX, 2, 16, 128)
        facts[x] = fact[x]
        for dx in range(1, NX):
            px = (x + dx) % NX
            cp = remote(fact.at[px], facts.at[x], n_send.at[dx], n_recv.at[dx], dev(y, c, z, px))
            cp.start()
            note_copies.append(cp)

    stack_heads(queries[...], stacked)
    acc[...] = jnp.zeros_like(acc)
    total[...] = jnp.zeros_like(total)
    for cp in ask_copies:
        cp.wait()
    cp = pltpu.make_async_copy(asks, ask_smem, l_sem)
    cp.start()
    cp.wait()
    sent = []

    def serve(zo, shard):
        row = pl.ds(pl.multiple_of(c * 32, 32), 32)
        for j, (px, pc) in enumerate(group):
            tile = jnp.clip(ask_smem[px * 2 + pc, zo * NX + x, 0], 0, 7)
            if j == 0:
                keys[zo * NX + x, row] = shard[tile]
                continue
            stage[j, zo] = shard[tile]
            cp = remote(
                stage.at[j, zo], keys.at[zo * NX + x, row], x_send.at[j, zo], x_recv.at[j, zo],
                dev(y, pc, z, px),
            )
            cp.start()
            sent.append(cp)

    def arrived(zo):
        for j in range(1, 8):
            row = pl.ds(0, 32)
            remote(
                stage.at[j, zo], keys.at[zo * NX, row], x_send.at[j, zo], x_recv.at[j, zo], right
            ).wait_recv()

    def attend(zo):
        w = weight_block(tile_weight[zo, 0:NX])

        def pair(p, carry):
            lanes = pl.ds(pl.multiple_of(p * 128, 128), 128)
            k = keys[pl.ds(zo * NX, NX), :, lanes].reshape(256, 128)
            capped = jnp.tanh(nt(k, stacked[p]) * (1.0 / 80.0))
            raw = w * jnp.exp2(capped * (10.0 * LOG2E))
            total[p] = total[p] + jnp.sum(raw, axis=0, keepdims=True)
            acc[p] = acc[p] + tn(k, raw.astype(BF16))
            return carry

        lax.fori_loop(0, PAIRS, pair, 0)

    def wait_step(way, step, k):
        ring[way, step, k].wait_recv()

    serve(z, half)
    pending = [z]
    for step in range(1, 4):
        for k in range(4):
            for way in (0, 1):
                wait_step(way, step - 1, k)
                if step < 3 or (k < 2) == (way == 0):
                    ring_send(way, step, k)
        serve((z + NZ - step) % NZ, slots[0][step])
        serve((z + step) % NZ, slots[1][step])
        for zo in pending:
            arrived(zo)
            attend(zo)
        if step == 1:
            slots_and_facts()
        pending = [(z + NZ - step) % NZ, (z + step) % NZ]
    for k in range(4):
        wait_step(0 if k < 2 else 1, 3, k)
    serve((z + 4) % NZ, far)
    for zo in pending:
        arrived(zo)
        attend(zo)
    arrived((z + 4) % NZ)
    attend((z + 4) % NZ)
    for p in range(PAIRS):
        mixed_t[p] = unstack_heads(acc[p] / total[p])
    mixed = jnp.concatenate([mixed_t[p].T for p in range(PAIRS)], axis=1).astype(BF16)
    aug[...] = (queries[...].astype(F32) + nn(mixed, out_proj[...])).astype(BF16)
    return list(ring.values()) + sent + note_copies


def labels_kernel(
    aug, onehot, facts, fact, n_send, n_recv, labels,
    d_aug, loss, label_step,
    rows, served, got, back, back_got, lstage, lgot, dlogit, lpart, lsend, lrecv,
    psend, prbuf, label_grad, label_got,
    z_send, z_recv, x_send, x_recv, b_send, b_recv, s_send, s_recv, p_send, p_recv, q_send, q_recv,
    g_send, g_recv,
):
    y, c, z, x = where_am_i()
    dp = y * 2 + c
    right, left = dev(y, c, (z + 1) % NZ, x), dev(y, c, (z + NZ - 1) % NZ, x)
    ring = {}

    def ring_send(way, step, k):
        own = (z + NZ - step) % NZ if way == 0 else (z + step) % NZ
        piece = pl.ds(k * 32, 32)
        src = aug.at[piece] if step == 0 else rows.at[own, piece]
        cp = remote(
            src, rows.at[own, piece], z_send.at[way, step, k], z_recv.at[way, step, k],
            right if way == 0 else left,
        )
        cp.start()
        ring[way, step, k] = cp

    for k in range(4):
        for way in (0, 1):
            ring_send(way, 0, k)
    rows[z] = aug[...]
    sent = []

    def serve(o):
        zs = (z + o) % NZ
        picked = tn(onehot[o], rows[zs]).astype(BF16)
        served[zs] = picked.reshape(NX, 2, 16, D)
        got[zs, :, x] = served[zs, x]
        for dx in range(1, NX):
            px = (x + dx) % NX
            cp = remote(
                served.at[zs, px], got.at[zs, :, x], x_send.at[dx, zs], x_recv.at[dx, zs],
                dev(y, c, z, px),
            )
            cp.start()
            sent.append(cp)

    label = lax.broadcasted_iota(jnp.int32, (64, 512), 1).astype(F32)
    lane = lax.broadcasted_iota(jnp.int32, (NX, 16, 128), 2)
    lstage[...] = jnp.zeros_like(lstage)

    def work(o):
        zs = (z + o) % NZ
        for dx in range(1, NX):
            remote(
                served.at[0, 0], got.at[zs, :, 0], x_send.at[dx, zs], x_recv.at[dx, zs], right
            ).wait_recv()

        def cluster(cl, carry):
            entries = got[zs, cl].reshape(64, D)
            logits = nt(entries, labels[cl])
            want = facts[:, cl].reshape(64, 128)
            first = o * 16
            live = want[:, first + 12 : first + 13]
            cluster_id = ((z * NX + x) * 2 + cl).astype(F32)
            hit = None
            for j in range(4):
                named = want[:, first + j : first + j + 1]
                high = want[:, first + 4 + j : first + 5 + j]
                low = want[:, first + 8 + j : first + 9 + j]
                one = label == jnp.where(named == cluster_id, high * 256.0 + low, -1.0)
                hit = one if hit is None else hit | one
            e = jnp.exp(-jnp.abs(logits))
            soft = jnp.maximum(logits, 0.0) + jnp.log1p(e)
            pair_loss = jnp.sum(soft - jnp.where(hit, logits, 0.0), axis=1, keepdims=True) * live
            inv = 1.0 / (1.0 + e)
            sig = jnp.where(logits >= 0, inv, 1.0 - inv)
            dl = ((sig - jnp.where(hit, 1.0, 0.0)) * live).astype(BF16)
            dlogit[zs, cl] = dl
            back[zs, cl] = nn(dl, labels[cl]).astype(BF16).reshape(NX, 16, D)
            spread = jnp.broadcast_to(pair_loss, (64, 128)).reshape(NX, 16, 128)
            lstage[:, cl] = jnp.where(lane == zs, spread, lstage[:, cl])
            return carry

        lax.fori_loop(0, 2, cluster, 0)

    def send_back(zs):
        back_got[zs, x] = back[zs, :, x]
        for dx in range(1, NX):
            px = (x + dx) % NX
            cp = remote(
                back.at[zs, :, px], back_got.at[zs, x], b_send.at[dx, zs], b_recv.at[dx, zs],
                dev(y, c, z, px),
            )
            cp.start()
            sent.append(cp)

    serve(0)
    for dx in range(1, NX):
        remote(fact.at[0], facts.at[0], n_send.at[dx], n_recv.at[dx], right).wait_recv()
    pending = [0]
    for step in range(1, 4):
        for k in range(4):
            for way in (0, 1):
                ring[way, step - 1, k].wait_recv()
                if step < 3 or (k < 2) == (way == 0):
                    ring_send(way, step, k)
        fresh = [NZ - step, step]
        for o in fresh:
            serve(o)
        for o in pending:
            work(o)
        pending = fresh
    for k in range(4):
        ring[0 if k < 2 else 1, 3, k].wait_recv()
    serve(4)
    for o in pending:
        work(o)
        send_back((z + o) % NZ)
    work(4)
    for d in (4, 2, 6, 1, 7, 0):
        send_back((z + d) % NZ)
    loss_copies = []
    for dx in range(1, NX):
        px = (x + dx) % NX
        cp = remote(lstage.at[px], lgot.at[x], s_send.at[dx], s_recv.at[dx], dev(y, c, z, px))
        cp.start()
        loss_copies.append(cp)
    lgot[x] = lstage[x]

    def partial(o):
        zs = (z + o) % NZ
        for dx in range(1, NX):
            remote(
                back.at[0, :, 0], back_got.at[zs, 0], b_send.at[dx, zs], b_recv.at[dx, zs], right
            ).wait_recv()
        return nn(onehot[o], back_got[zs].reshape(128, D))

    label_copies = []

    def label_part(cl):
        entries = got[:, cl].reshape(512, D)
        for part in range(2):
            columns = slice(part * 256, part * 256 + 256)
            value = tn(dlogit[:, cl, :, columns].reshape(512, 256), entries)
            label_grad[cl, part * 4 : part * 4 + 4] = value.astype(BF16).reshape(4, 64, D)
        label_got[cl, dp] = label_grad[cl, dp]
        for d in range(1, 8):
            to = (dp + d) % 8
            cp = remote(
                label_grad.at[cl, to], label_got.at[cl, dp], g_send.at[cl, d], g_recv.at[cl, d],
                (to, z * NX + x),
            )
            cp.start()
            label_copies.append(cp)

    p_copies = {}

    def chain_send(way, step, h, value):
        piece = pl.ds(h * 64, 64)
        psend[way, step, piece] = value.astype(BF16)
        cp = remote(
            psend.at[way, step, piece], prbuf.at[way, step, piece],
            p_send.at[way, step, h], p_recv.at[way, step, h], right if way == 0 else left,
        )
        cp.start()
        p_copies[way, step, h] = cp

    label_part(0)
    far = partial(4)
    for way in (0, 1):
        chain_send(way, 0, way, far[way * 64 : way * 64 + 64])
    label_part(1)
    for step in range(1, 4):
        d = 4 - step
        own = [partial(d), partial(NZ - d)]
        for h in (0, 1):
            for way in (h, 1 - h):
                value = own[way][h * 64 : h * 64 + 64]
                if (way, step - 1, h) in p_copies:
                    p_copies[way, step - 1, h].wait_recv()
                    value = value + prbuf[way, step - 1, h * 64 : h * 64 + 64].astype(F32)
                chain_send(way, step, h, value)
    mine = partial(0)
    for cp in loss_copies:
        cp.wait()
    losses = jnp.concatenate([lgot[i].reshape(32, 128) for i in range(NX)], axis=0).astype(BF16)
    out_lane = lax.broadcasted_iota(jnp.int32, (Q, 128), 1)
    lpart[...] = jnp.zeros_like(lpart)

    def loss_of(i, carry):
        lpart[...] = lpart[...] + jnp.where(out_lane == (z + i) % NZ, nn(onehot[i], losses), 0.0)
        return carry

    lax.fori_loop(0, NZ, loss_of, 0)
    lsend[...] = lpart[...].T[:NZ]
    l_copies = []
    for d in range(1, NZ):
        zp = (z + d) % NZ
        cp = remote(lsend, lrecv.at[z], q_send.at[d], q_recv.at[d], dev(y, c, zp, x))
        cp.start()
        l_copies.append(cp)
    lrecv[z] = lsend[...]
    for h in (0, 1):
        for way in (0, 1):
            p_copies[way, 3, h].wait_recv()
    d_aug[...] = mine + prbuf[0, 3].astype(F32) + prbuf[1, 3].astype(F32)
    for cp in l_copies:
        cp.wait()
    loss[...] = jnp.sum(lrecv[:, pl.ds(z, 1), :], axis=0) * (1.0 / 2048.0)
    for cp in label_copies:
        cp.wait()
    for cl in range(2):
        grad = label_got[cl, 0].astype(F32)
        for i in range(1, 8):
            grad = grad + label_got[cl, i].astype(F32)
        square = jnp.mean(grad * grad, axis=1, keepdims=True)
        label_step[cl] = grad * lax.rsqrt(square + epsilon)
    return list(p_copies.values()) + list(ring.values()) + sent


def grads_kernel(
    asks, keys, queries, d_aug, out_proj, mixed_t, total, tile_weight,
    query_grad, know_grad,
    stacked, d_acc, delta, gsend, ggot, ysend, ygot, zsend, zgot,
    x_send, x_recv, y_send, y_recv, z_send, z_recv,
):
    y, c, z, x = where_am_i()
    me = x * 2 + c
    group = [((x + dx) % NX, (c + dc) % 2) for dx, dc in XC]
    d_rows = d_aug[...]
    back_proj = nt(d_rows.astype(BF16), out_proj[...]).astype(BF16)
    stack_heads(queries[...], stacked.at[:, 0:256])
    stack_heads(back_proj, stacked.at[:, 256:512])
    for p in range(PAIRS):
        product = mixed_t[p] * back_proj[:, p * 128 : (p + 1) * 128].astype(F32).T
        delta[p] = jnp.concatenate(
            [
                jnp.sum(product[:64], axis=0, keepdims=True),
                jnp.sum(product[64:], axis=0, keepdims=True),
            ],
            axis=1,
        )
    d_acc[...] = jnp.zeros_like(d_acc)

    def compute(zo):
        w = weight_block(tile_weight[zo, 0:NX])

        def pair(p, carry):
            lanes = pl.ds(pl.multiple_of(p * 128, 128), 128)
            k = keys[pl.ds(zo * NX, NX), :, lanes].reshape(256, 128)
            rows = stacked[p]
            products = nt(k, rows)
            capped = jnp.tanh(products[:, :256] * (1.0 / 80.0))
            soft = w * jnp.exp2(capped * (10.0 * LOG2E)) * (1.0 / total[p])
            d_score = soft * (products[:, 256:] - delta[p]) * ((1.0 - capped * capped) * 0.125)
            both = jnp.concatenate([d_score.astype(BF16), soft.astype(BF16)], axis=1)
            d_acc[p] = d_acc[p] + tn(k, both[:, :256])
            grad = nn(both, rows).reshape(NX, NY, 2, 8, 128)
            for side in range(2):
                gsend[zo, :, side, :, lanes] = grad[:, :, side].reshape(NX, 32, 128).astype(BF16)
            return carry

        lax.fori_loop(0, PAIRS, pair, 0)
        ggot[me, zo] = gsend[zo, x, c]
        for j in range(1, 8):
            px, pc = group[j]
            remote(
                gsend.at[zo, px, pc], ggot.at[me, zo], x_send.at[j, zo], x_recv.at[j, zo],
                dev(y, pc, z, px),
            ).start()

    def gather_tiles(zo):
        for j in range(1, 8):
            remote(
                gsend.at[zo, 0, 0], ggot.at[0, zo], x_send.at[j, zo], x_recv.at[j, zo],
                dev(y, c, z, x),
            ).wait_recv()
        tiles = [asks[s, zo * NX + x, 0] for s in range(8)]

        def two_tiles(k2, carry):
            sums = []
            for k in range(2):
                value = jnp.zeros((32, D), F32)
                for s in range(8):
                    value = value + ggot[s, zo].astype(F32) * jnp.where(
                        tiles[s] == k2 * 2 + k, 1.0, 0.0
                    )
                sums.append(value.reshape(NY, 1, 8, D))
            joined = jnp.concatenate(sums, axis=1).reshape(NY, 16, D).astype(BF16)
            ysend[zo, :, k2] = joined
            return carry

        lax.fori_loop(0, 4, two_tiles, 0)
        ygot[y, zo] = ysend[zo, y]
        for d in range(1, NY):
            py = (y + d) % NY
            remote(
                ysend.at[zo, py], ygot.at[y, zo], y_send.at[d, zo], y_recv.at[d, zo],
                dev(py, c, z, x),
            ).start()

    def gather_shards(zo, own):
        for d in range(1, NY):
            remote(
                ysend.at[zo, 0], ygot.at[0, zo], y_send.at[d, zo], y_recv.at[d, zo],
                dev(y, c, z, x),
            ).wait_recv()
        value = ygot[0, zo].astype(F32)
        for i in range(1, NY):
            value = value + ygot[i, zo].astype(F32)
        zsend[zo] = value.astype(BF16)

        @pl.when(own == 0)
        def _():
            zgot[z] = zsend[z]

        @pl.when(own != 0)
        def _():
            remote(
                zsend.at[zo], zgot.at[z], z_send.at[own], z_recv.at[own], dev(y, c, zo, x)
            ).start()

    def offset(i):
        return (3 * (i + 1)) % NZ

    def body(i, carry):
        @pl.when(i < 8)
        def _():
            compute((z + offset(i)) % NZ)

        @pl.when((i >= 3) & (i < 11))
        def _():
            gather_tiles((z + offset(i - 3)) % NZ)

        @pl.when(i >= 5)
        def _():
            gather_shards((z + offset(i - 5)) % NZ, offset(i - 5))

        return carry

    lax.fori_loop(0, 13, body, 0)
    d_query = jnp.concatenate([unstack_heads(d_acc[p]).T for p in range(PAIRS)], axis=1)
    query_grad[...] = d_rows + d_query
    for d in range(1, NZ):
        remote(zsend.at[0], zgot.at[0], z_send.at[d], z_recv.at[d], dev(y, c, z, x)).wait_recv()
    value = zgot[0].astype(F32)
    for i in range(1, NZ):
        value = value + zgot[i].astype(F32)
    know_grad[...] = value.reshape(8, 8, D)

    def drain(zo, carry):
        for j in range(1, 8):
            remote(
                gsend.at[zo, 0, 0], ggot.at[0, zo], x_send.at[j, zo], x_recv.at[j, zo],
                dev(y, c, z, x),
            ).wait_send()
        for d in range(1, NY):
            remote(
                ysend.at[zo, 0], ygot.at[0, zo], y_send.at[d, zo], y_recv.at[d, zo],
                dev(y, c, z, x),
            ).wait_send()
        return carry

    lax.fori_loop(0, NZ, drain, 0)
    for d in range(1, NZ):
        remote(zsend.at[0], zgot.at[0], z_send.at[d], z_recv.at[d], dev(y, c, z, x)).wait_send()


V = pl.BlockSpec(memory_space=pltpu.VMEM)


def scratch():
    names = dict(
        keys=((32, 64, D), BF16), aug=((Q, D), BF16), mixed_t=((PAIRS, 128, Q), F32),
        total=((PAIRS, 1, 2 * Q), F32), tile_weight=((NZ, 8, Q), F32), onehot=((NZ, Q, 128), BF16),
        facts=((NX, 2, 16, 128), F32), ask_smem=None,
        wanted=((32, 128), jnp.int32), asks=((8, 32, 128), jnp.int32),
        half=((8, 32, D), BF16), r0=((8, 32, D), BF16), r1=((8, 32, D), BF16),
        r2=((8, 32, D), BF16), l0=((8, 32, D), BF16), l1=((8, 32, D), BF16),
        l2=((8, 32, D), BF16), far=((8, 32, D), BF16), stage=((8, NZ, 32, D), BF16),
        stacked=((PAIRS, 2 * Q, 128), BF16), acc=((PAIRS, 128, 2 * Q), F32),
        note=((NZ, 24, 128), F32), noted=((NZ, 24, 128), F32), fact=((NX, 2, 16, 128), F32),
    )
    first = [
        pltpu.SMEM((8, 32, 128), jnp.int32) if v is None else pltpu.VMEM(*v)
        for v in names.values()
    ]
    first += [
        DMA(n)
        for n in ((2, 4, 4), (2, 4, 4), (8, NZ), (8, NZ), (8,), (8,), (NZ,), (NZ,), (NX,), (NX,))
    ] + [DMA]
    second = [
        pltpu.VMEM((Q, D), F32),
        pltpu.VMEM((NZ, Q, D), BF16),
        pltpu.VMEM((NZ, NX, 2, 16, D), BF16),
        pltpu.VMEM((NZ, 2, NX, 16, D), BF16),
        pltpu.VMEM((NZ, 2, NX, 16, D), BF16),
        pltpu.VMEM((NZ, NX, 2, 16, D), BF16),
        pltpu.VMEM((NX, 2, 16, 128), F32),
        pltpu.VMEM((NX, 2, 16, 128), F32),
        pltpu.VMEM((NZ, 2, 64, 512), BF16),
        pltpu.VMEM((Q, 128), F32),
        pltpu.VMEM((NZ, 128), F32),
        pltpu.VMEM((NZ, NZ, 128), F32),
        pltpu.VMEM((2, 4, Q, D), BF16),
        pltpu.VMEM((2, 4, Q, D), BF16),
        pltpu.VMEM((2, 8, 64, D), BF16),
        pltpu.VMEM((2, 8, 64, D), BF16),
    ] + [
        DMA(n)
        for n in (
            (2, 4, 4), (2, 4, 4), (NX, NZ), (NX, NZ), (NX, NZ), (NX, NZ), (NX,), (NX,),
            (2, 4, 2), (2, 4, 2), (NZ,), (NZ,), (2, 8), (2, 8),
        )
    ]
    third = [
        pltpu.VMEM((PAIRS, 4 * Q, 128), BF16),
        pltpu.VMEM((PAIRS, 128, 2 * Q), F32),
        pltpu.VMEM((PAIRS, 1, 2 * Q), F32),
        pltpu.VMEM((NZ, NX, 2, 32, D), BF16),
        pltpu.VMEM((8, NZ, 32, D), BF16),
        pltpu.VMEM((NZ, NY, 4, 16, D), BF16),
        pltpu.VMEM((NY, NZ, 4, 16, D), BF16),
        pltpu.VMEM((NZ, 4, 16, D), BF16),
        pltpu.VMEM((NZ, 4, 16, D), BF16),
    ] + [DMA(n) for n in ((8, NZ), (8, NZ), (NY, NZ), (NY, NZ), (NZ,), (NZ,))]
    return first, second, third


def whole_kernel(*refs):
    sizes = [len(part) for part in scratch()]
    know, numbers, queries, out_proj, labels, loss, query_grad, know_grad, label_step = refs[:9]
    first = refs[9 : 9 + sizes[0]]
    second = refs[9 + sizes[0] : 9 + sizes[0] + sizes[1]]
    third = refs[9 + sizes[0] + sizes[1] :]
    keys, aug, mixed_t, total, tile_weight, onehot, facts, ask_smem = first[:8]
    fact, n_send, n_recv = first[23], first[32], first[33]
    sends = keys_kernel(know, numbers, queries, out_proj, *first)
    d_aug = second[0]
    sends += labels_kernel(
        aug, onehot, facts, fact, n_send, n_recv, labels, d_aug, loss, label_step, *second[1:]
    )
    grads_kernel(
        ask_smem, keys, queries, d_aug, out_proj, mixed_t, total, tile_weight,
        query_grad, know_grad, *third,
    )
    for cp in sends:
        cp.wait_send()


def on_device(queries, tile_ids, knowledge, out_proj, labels, cluster_ids, positive_picks):
    numbers = jnp.concatenate([tile_ids, cluster_ids, positive_picks], axis=1).T
    first, second, third = scratch()
    loss, query_grad, knowledge_grad, label_step = pl.pallas_call(
        whole_kernel,
        out_shape=[
            jax.ShapeDtypeStruct((1, Q), F32),
            jax.ShapeDtypeStruct((Q, D), F32),
            jax.ShapeDtypeStruct((8, 8, D), F32),
            jax.ShapeDtypeStruct((2, 64, D), F32),
        ],
        in_specs=[V] * 5,
        out_specs=[V] * 4,
        scratch_shapes=first + second + third,
        compiler_params=pltpu.CompilerParams(
            collective_id=1, has_side_effects=True, vmem_limit_bytes=VMEM_LIMIT
        ),
    )(knowledge, numbers, queries, out_proj, labels)
    return (loss[0], query_grad, knowledge_grad, label_step)


def solution(mesh):
    placed = (
        P(("dp", "table"), None),
        P(("dp", "table"), None),
        P("table", None, None),
        P(),
        P("table", None, None),
        P(("dp", "table"), None),
        P(("dp", "table"), None),
    )
    return jax.shard_map(
        on_device,
        mesh=mesh,
        in_specs=placed,
        out_specs=(
            P(("dp", "table")),
            P(("dp", "table"), None),
            P("table", "dp", None),
            P("table", "dp", None),
        ),
        check_vma=False,
    )
```

```python
import jax
import jax.numpy as jnp
from jax import lax
from jax.experimental import pallas as pl
from jax.experimental.pallas import tpu as pltpu
from jax.sharding import PartitionSpec as P

MESH = pl.DeviceIdType.MESH
DMA = pltpu.SemaphoreType.DMA
F32 = jnp.float32
BF16 = jnp.bfloat16
PAIRS = 6
Q = 128
D = 768
NZ = 8
NX = 4
NY = 4
epsilon = 1e-06
LOG2E = 1.4426950408889634
VMEM_LIMIT = 56 << 20


def where_am_i():
    dp, t = lax.axis_index("dp"), lax.axis_index("table")
    return dp // 2, dp % 2, t // NX, t % NX


def dev(y, c, z, x):
    return (y * 2 + c, z * NX + x)


def greet(peers):
    barrier = pltpu.get_barrier_semaphore()
    for peer in peers:
        pl.semaphore_signal(barrier, inc=1, device_id=peer, device_id_type=MESH)
    return lambda: pl.semaphore_wait(barrier, len(peers))


def remote(src, dst, send, recv, to):
    return pltpu.make_async_remote_copy(
        src_ref=src, dst_ref=dst, send_sem=send, recv_sem=recv, device_id=to, device_id_type=MESH
    )


def nt(a, b):
    return lax.dot_general(a, b, (((1,), (1,)), ((), ())), preferred_element_type=F32)


def tn(a, b):
    return lax.dot_general(a, b, (((0,), (0,)), ((), ())), preferred_element_type=F32)


def nn(a, b):
    return jnp.dot(a, b, preferred_element_type=F32)


def stack_heads(rows, stacked_ref):
    lane = lax.broadcasted_iota(jnp.int32, (Q, 128), 1)
    for p in range(PAIRS):
        part = rows[:, p * 128 : (p + 1) * 128]
        stacked_ref[p, :Q] = jnp.where(lane < 64, part, jnp.zeros_like(part))
        stacked_ref[p, Q:] = jnp.where(lane < 64, jnp.zeros_like(part), part)


def unstack_heads(both):
    return jnp.concatenate([both[0:64, 0:Q], both[64:128, Q : 2 * Q]], axis=0)


def weight_block(tw):
    tw2 = jnp.concatenate([tw, tw], axis=1)
    return jnp.broadcast_to(tw2[:, None, :], (NX, 64, 2 * Q)).reshape(NX * 64, 2 * Q)


XC = [(dx, dc) for dx in range(NX) for dc in range(2)]


def keys_kernel(
    know, numbers, queries, out_proj,
    keys, aug, mixed_t, total, tile_weight, onehot, facts, ask_smem,
    wanted, asks, ask_row,
    half0, half1, r00, r01, r10, r11, r20, r21, l00, l01, l10, l11, l20, l21, far0, far1,
    stage, stacked, acc, note, noted, fact,
    z_send, z_recv, x_send, x_recv, a_send, a_recv, m_send, m_recv, n_send, n_recv, l_sem,
):
    y, c, z, x = where_am_i()
    dp = y * 2 + c
    me = x * 2 + c
    start, far = (half0, half1), (far0, far1)
    r0, r1, r2 = (r00, r01), (r10, r11), (r20, r21)
    l0, l1, l2 = (l00, l01), (l10, l11), (l20, l21)
    right, left = dev(y, c, (z + 1) % NZ, x), dev(y, c, (z + NZ - 1) % NZ, x)
    group = [((x + dx) % NX, (c + dc) % 2) for dx, dc in XC]
    everyone_in = greet(
        [dev(y, pc, z, px) for px, pc in group[1:]]
        + [dev(y, c, (z + d) % NZ, x) for d in range(1, NZ)]
        + [((dp + d) % 8, z * NX + x) for d in range(1, 8)]
    )
    for h in (0, 1):
        start[h][...] = know[:, pl.ds(pl.multiple_of(c * 32 + h * 16, 16), 16), :]
    owner = lax.broadcasted_iota(jnp.int32, (32, Q), 0)
    weight, tile = jnp.zeros((32, Q), F32), jnp.zeros((32, Q), jnp.int32)
    for r in range(4):
        named = numbers[r : r + 1, :]
        hit = (named >> 3) == owner
        weight = weight + jnp.where(hit, 1.0, 0.0)
        tile = jnp.maximum(tile, jnp.where(hit, named & 7, 0))
    tile = jnp.broadcast_to(jnp.max(tile, axis=1, keepdims=True), (32, 128)).reshape(NZ, NX, 128)
    for i in range(NX):
        wanted[i] = tile[:, i]
    ask_copies = []
    asks[me] = wanted[x]
    for zo in range(NZ):
        tile_weight[zo, 0:NX] = weight[zo * NX : zo * NX + NX]
    cluster = lax.broadcasted_iota(jnp.int32, (64, Q), 0)
    ids = [numbers[4 + i : 5 + i, :] for i in range(4)]
    member = ids[0] == cluster
    for i in range(1, 4):
        member = member | (ids[i] == cluster)
    row = lax.broadcasted_iota(jnp.int32, (Q, 128), 0)
    lane = lax.broadcasted_iota(jnp.int32, (Q, 128), 1)
    before = jnp.where(row < lane, 1.0, 0.0).astype(BF16)
    rank = nn(jnp.where(member, 1.0, 0.0).astype(BF16), before)
    rank = jnp.where(member, rank, -1.0)
    picks = [numbers[8 + j : 9 + j, :] for j in range(4)]
    columns = []
    for j in range(4):
        column = picks[j] >> 9
        named = jnp.where(column == 0, ids[0], 0)
        for i in range(1, 4):
            named = jnp.where(column == i, ids[i], named)
        columns.append(named)
    columns += [(pick & 511) >> 8 for pick in picks] + [pick & 255 for pick in picks]
    columns += [jnp.ones_like(picks[0])] + [jnp.zeros_like(picks[0])] * 3
    columns = jnp.concatenate(columns, axis=0).astype(F32)
    for i in range(NZ):
        note[i, 0:8] = rank[i * 8 : i * 8 + 8]
        note[i, 8:24] = columns
    stack_heads(queries[...], stacked)
    acc[...] = jnp.zeros_like(acc)
    total[...] = jnp.zeros_like(total)
    everyone_in()
    for j in range(1, 8):
        px, pc = group[j]
        cp = remote(wanted.at[px], asks.at[me], a_send.at[j], a_recv.at[j], dev(y, pc, z, px))
        cp.start()
        ask_copies.append(cp)
    ring = {}
    slots = ((start, r0, r1, r2, far), (start, l0, l1, l2, far))

    def ring_send(way, step, k):
        h, piece = k // 2, pl.ds((k % 2) * 4, 4)
        cp = remote(
            slots[way][step][h].at[piece], slots[way][step + 1][h].at[piece],
            z_send.at[way, step, k], z_recv.at[way, step, k], right if way == 0 else left,
        )
        cp.start()
        ring[way, step, k] = cp

    for k in range(4):
        for way in (0, 1):
            ring_send(way, 0, k)
    note_copies = []
    for d in range(1, NZ):
        zp = (z + d) % NZ
        cp = remote(
            note.at[zp], noted.at[NZ - d], m_send.at[d], m_recv.at[NZ - d], dev(y, c, zp, x)
        )
        cp.start()
        note_copies.append(cp)
    noted[0] = note[z]

    def slots_and_facts():
        for d in range(1, NZ):
            remote(note.at[0], noted.at[d], m_send.at[d], m_recv.at[d], right).wait_recv()
        spread = jnp.where(
            lax.broadcasted_iota(jnp.int32, (16, 128), 0)
            == lax.broadcasted_iota(jnp.int32, (16, 128), 1) // 16,
            1.0, 0.0,
        ).astype(BF16)
        place = (lane % 16).astype(F32)
        about = noted[:, 8:24, :].reshape(128, Q).T
        value = jnp.zeros((128, 128), F32)
        for o in range(NZ):
            hot = jnp.where(tn(noted[o, 0:16].astype(BF16), spread) == place, 1.0, 0.0).astype(BF16)
            onehot[o] = hot
            value = value + tn(hot, jnp.where(lane // 16 == o, about, 0.0).astype(BF16))
        fact[...] = value.reshape(NX, 2, 16, 128)
        facts[x] = fact[x]
        for dx in range(1, NX):
            px = (x + dx) % NX
            cp = remote(fact.at[px], facts.at[x], n_send.at[dx], n_recv.at[dx], dev(y, c, z, px))
            cp.start()
            note_copies.append(cp)

    for cp in ask_copies:
        cp.wait()
    peer = lax.broadcasted_iota(jnp.int32, (NZ, 128), 1)
    table = jnp.zeros((NZ, 128), jnp.int32)
    for i in range(8):
        table = jnp.where(peer == i, asks[i], table)
    ask_row[...] = table
    cp = pltpu.make_async_copy(ask_row, ask_smem, l_sem)
    cp.start()
    cp.wait()

    def serve(zo, h, shard):
        row = pl.ds(pl.multiple_of(c * 32 + h * 16, 16), 16)
        for j, (px, pc) in enumerate(group):
            tile = jnp.clip(ask_smem[zo, px * 2 + pc], 0, 7)
            if j == 0:
                keys[zo * NX + x, row] = shard[tile]
                continue
            stage[j, zo, h] = shard[tile]
            cp = remote(
                stage.at[j, zo, h], keys.at[zo * NX + x, row], x_send.at[0],
                x_recv.at[zo], dev(y, pc, z, px),
            )
            cp.start()

    def arrived(zo):
        pieces = stage.at[pl.ds(0, 7), zo]
        remote(pieces, pieces, x_send.at[0], x_recv.at[zo], right).wait_recv()

    def attend(zo):
        w = weight_block(tile_weight[zo, 0:NX])

        def pair(p, carry):
            lanes = pl.ds(pl.multiple_of(p * 128, 128), 128)
            k = keys[pl.ds(zo * NX, NX), :, lanes].reshape(256, 128)
            capped = jnp.tanh(nt(k, stacked[p]) * (1.0 / 80.0))
            raw = w * jnp.exp2(capped * (10.0 * LOG2E))
            total[p] = total[p] + jnp.sum(raw, axis=0, keepdims=True)
            acc[p] = acc[p] + tn(k, raw.astype(BF16))
            return carry

        lax.fori_loop(0, PAIRS, pair, 0)

    def wait_step(way, step, k):
        ring[way, step, k].wait_recv()

    for h in (0, 1):
        serve(z, h, start[h])
    pending = [z]
    for step in range(1, 4):
        fresh = [(z + NZ - step) % NZ, (z + step) % NZ]
        for h in (0, 1):
            for k in (2 * h, 2 * h + 1):
                for way in (0, 1):
                    wait_step(way, step - 1, k)
                    if step < 3 or (k < 2) == (way == 0):
                        ring_send(way, step, k)
            for way in (0, 1):
                serve(fresh[way], h, slots[way][step][h])
        for zo in pending:
            arrived(zo)
            attend(zo)
        if step == 1:
            slots_and_facts()
        pending = fresh
    for h in (0, 1):
        for k in (2 * h, 2 * h + 1):
            wait_step(h, 3, k)
        serve((z + 4) % NZ, h, far[h])
    for zo in pending:
        arrived(zo)
        attend(zo)
    arrived((z + 4) % NZ)
    attend((z + 4) % NZ)
    for p in range(PAIRS):
        mixed_t[p] = unstack_heads(acc[p] / total[p])
    mixed = jnp.concatenate([mixed_t[p].T for p in range(PAIRS)], axis=1).astype(BF16)
    aug[...] = (queries[...].astype(F32) + nn(mixed, out_proj[...])).astype(BF16)
    pieces = stage.at[pl.ds(0, 7)]
    return list(ring.values()) + [remote(pieces, pieces, x_send.at[0], x_recv.at[0], right)] + note_copies


def labels_kernel(
    aug, onehot, facts, fact, n_send, n_recv, labels,
    d_aug, loss, label_step,
    rows, served, got, back, back_got, lstage, lgot, dlogit, lpart, lsend, lrecv,
    psend, prbuf, label_grad, label_got,
    z_send, z_recv, x_send, x_recv, b_send, b_recv, s_send, s_recv, p_send, p_recv, q_send, q_recv,
    g_send, g_recv,
):
    y, c, z, x = where_am_i()
    dp = y * 2 + c
    right, left = dev(y, c, (z + 1) % NZ, x), dev(y, c, (z + NZ - 1) % NZ, x)
    ring = {}

    def ring_send(way, step, k):
        own = (z + NZ - step) % NZ if way == 0 else (z + step) % NZ
        piece = pl.ds(k * 32, 32)
        src = aug.at[piece] if step == 0 else rows.at[own, piece]
        cp = remote(
            src, rows.at[own, piece], z_send.at[way, step, k], z_recv.at[way, step, k],
            right if way == 0 else left,
        )
        cp.start()
        ring[way, step, k] = cp

    for k in range(4):
        for way in (0, 1):
            ring_send(way, 0, k)
    rows[z] = aug[...]
    sent = []

    def serve(o):
        zs = (z + o) % NZ
        picked = tn(onehot[o], rows[zs]).astype(BF16)
        served[zs] = picked.reshape(NX, 2, 16, D)
        got[zs, :, x] = served[zs, x]
        for dx in range(1, NX):
            px = (x + dx) % NX
            cp = remote(
                served.at[zs, px], got.at[zs, :, x], x_send.at[dx, zs], x_recv.at[dx, zs],
                dev(y, c, z, px),
            )
            cp.start()
            sent.append(cp)

    label = lax.broadcasted_iota(jnp.int32, (64, 512), 1).astype(F32)
    lane = lax.broadcasted_iota(jnp.int32, (NX, 16, 128), 2)
    lstage[...] = jnp.zeros_like(lstage)

    def work(o):
        zs = (z + o) % NZ
        for dx in range(1, NX):
            remote(
                served.at[0, 0], got.at[zs, :, 0], x_send.at[dx, zs], x_recv.at[dx, zs], right
            ).wait_recv()

        def cluster(cl, carry):
            entries = got[zs, cl].reshape(64, D)
            logits = nt(entries, labels[cl])
            want = facts[:, cl].reshape(64, 128)
            first = o * 16
            live = want[:, first + 12 : first + 13]
            cluster_id = ((z * NX + x) * 2 + cl).astype(F32)
            hit = None
            for j in range(4):
                named = want[:, first + j : first + j + 1]
                high = want[:, first + 4 + j : first + 5 + j]
                low = want[:, first + 8 + j : first + 9 + j]
                one = label == jnp.where(named == cluster_id, high * 256.0 + low, -1.0)
                hit = one if hit is None else hit | one
            e = jnp.exp(-jnp.abs(logits))
            soft = jnp.maximum(logits, 0.0) + jnp.log1p(e)
            pair_loss = jnp.sum(soft - jnp.where(hit, logits, 0.0), axis=1, keepdims=True) * live
            inv = 1.0 / (1.0 + e)
            sig = jnp.where(logits >= 0, inv, 1.0 - inv)
            dl = ((sig - jnp.where(hit, 1.0, 0.0)) * live).astype(BF16)
            dlogit[zs, cl] = dl
            back[zs, cl] = nn(dl, labels[cl]).astype(BF16).reshape(NX, 16, D)
            spread = jnp.broadcast_to(pair_loss, (64, 128)).reshape(NX, 16, 128)
            lstage[:, cl] = jnp.where(lane == zs, spread, lstage[:, cl])
            return carry

        lax.fori_loop(0, 2, cluster, 0)

    def send_back(zs):
        back_got[zs, x] = back[zs, :, x]
        for dx in range(1, NX):
            px = (x + dx) % NX
            cp = remote(
                back.at[zs, :, px], back_got.at[zs, x], b_send.at[dx, zs], b_recv.at[dx, zs],
                dev(y, c, z, px),
            )
            cp.start()
            sent.append(cp)

    serve(0)
    for dx in range(1, NX):
        remote(fact.at[0], facts.at[0], n_send.at[dx], n_recv.at[dx], right).wait_recv()
    pending = [0]
    for step in range(1, 4):
        for k in range(4):
            for way in (0, 1):
                ring[way, step - 1, k].wait_recv()
                if step < 3 or (k < 2) == (way == 0):
                    ring_send(way, step, k)
        fresh = [NZ - step, step]
        for o in fresh:
            serve(o)
        for o in pending:
            work(o)
        pending = fresh
    for k in range(4):
        ring[0 if k < 2 else 1, 3, k].wait_recv()
    serve(4)
    for o in pending:
        work(o)
        send_back((z + o) % NZ)
    work(4)
    for d in (4, 2, 6, 1, 7, 0):
        send_back((z + d) % NZ)
    loss_copies = []
    for dx in range(1, NX):
        px = (x + dx) % NX
        cp = remote(lstage.at[px], lgot.at[x], s_send.at[dx], s_recv.at[dx], dev(y, c, z, px))
        cp.start()
        loss_copies.append(cp)
    lgot[x] = lstage[x]

    def partial(o):
        zs = (z + o) % NZ
        for dx in range(1, NX):
            remote(
                back.at[0, :, 0], back_got.at[zs, 0], b_send.at[dx, zs], b_recv.at[dx, zs], right
            ).wait_recv()
        return nn(onehot[o], back_got[zs].reshape(128, D))

    label_copies = []

    def label_part(cl):
        entries = got[:, cl].reshape(512, D)
        for part in range(2):
            columns = slice(part * 256, part * 256 + 256)
            value = tn(dlogit[:, cl, :, columns].reshape(512, 256), entries)
            label_grad[cl, part * 4 : part * 4 + 4] = value.astype(BF16).reshape(4, 64, D)
        label_got[cl, dp] = label_grad[cl, dp]
        for d in range(1, 8):
            to = (dp + d) % 8
            cp = remote(
                label_grad.at[cl, to], label_got.at[cl, dp], g_send.at[cl, d], g_recv.at[cl, d],
                (to, z * NX + x),
            )
            cp.start()
            label_copies.append(cp)

    p_copies = {}

    def chain_send(way, step, h, value):
        piece = pl.ds(h * 64, 64)
        psend[way, step, piece] = value.astype(BF16)
        cp = remote(
            psend.at[way, step, piece], prbuf.at[way, step, piece],
            p_send.at[way, step, h], p_recv.at[way, step, h], right if way == 0 else left,
        )
        cp.start()
        p_copies[way, step, h] = cp

    label_part(0)
    far = partial(4)
    for way in (0, 1):
        chain_send(way, 0, way, far[way * 64 : way * 64 + 64])
    label_part(1)
    for step in range(1, 4):
        d = 4 - step
        own = [partial(d), partial(NZ - d)]
        for h in (0, 1):
            for way in (h, 1 - h):
                value = own[way][h * 64 : h * 64 + 64]
                if (way, step - 1, h) in p_copies:
                    p_copies[way, step - 1, h].wait_recv()
                    value = value + prbuf[way, step - 1, h * 64 : h * 64 + 64].astype(F32)
                chain_send(way, step, h, value)
    mine = partial(0)
    for cp in loss_copies:
        cp.wait()
    losses = jnp.concatenate([lgot[i].reshape(32, 128) for i in range(NX)], axis=0).astype(BF16)
    out_lane = lax.broadcasted_iota(jnp.int32, (Q, 128), 1)
    lpart[...] = jnp.zeros_like(lpart)

    def loss_of(i, carry):
        lpart[...] = lpart[...] + jnp.where(out_lane == (z + i) % NZ, nn(onehot[i], losses), 0.0)
        return carry

    lax.fori_loop(0, NZ, loss_of, 0)
    lsend[...] = lpart[...].T[:NZ]
    l_copies = []
    for d in range(1, NZ):
        zp = (z + d) % NZ
        cp = remote(lsend, lrecv.at[z], q_send.at[d], q_recv.at[d], dev(y, c, zp, x))
        cp.start()
        l_copies.append(cp)
    lrecv[z] = lsend[...]
    for h in (0, 1):
        for way in (0, 1):
            p_copies[way, 3, h].wait_recv()
    d_aug[...] = mine + prbuf[0, 3].astype(F32) + prbuf[1, 3].astype(F32)
    for cp in l_copies:
        cp.wait()
    loss[...] = jnp.sum(lrecv[:, pl.ds(z, 1), :], axis=0) * (1.0 / 2048.0)
    for cp in label_copies:
        cp.wait()
    for cl in range(2):
        grad = label_got[cl, 0].astype(F32)
        for i in range(1, 8):
            grad = grad + label_got[cl, i].astype(F32)
        square = jnp.mean(grad * grad, axis=1, keepdims=True)
        label_step[cl] = grad * lax.rsqrt(square + epsilon)
    return list(p_copies.values()) + list(ring.values()) + sent


def grads_kernel(
    asks, keys, queries, d_aug, out_proj, mixed_t, total, tile_weight,
    query_grad, know_grad,
    stacked, d_acc, delta, gsend, ggot, ysend, ygot, zsend, zgot,
    x_send, x_recv, y_send, y_recv, z_send, z_recv,
):
    y, c, z, x = where_am_i()
    me = x * 2 + c
    group = [((x + dx) % NX, (c + dc) % 2) for dx, dc in XC]
    d_rows = d_aug[...]
    back_proj = nt(d_rows.astype(BF16), out_proj[...]).astype(BF16)
    stack_heads(queries[...], stacked.at[:, 0:256])
    stack_heads(back_proj, stacked.at[:, 256:512])
    for p in range(PAIRS):
        product = mixed_t[p] * back_proj[:, p * 128 : (p + 1) * 128].astype(F32).T
        delta[p] = jnp.concatenate(
            [
                jnp.sum(product[:64], axis=0, keepdims=True),
                jnp.sum(product[64:], axis=0, keepdims=True),
            ],
            axis=1,
        )
    d_acc[...] = jnp.zeros_like(d_acc)

    def compute(zo):
        w = weight_block(tile_weight[zo, 0:NX])

        def pair(p, carry):
            lanes = pl.ds(pl.multiple_of(p * 128, 128), 128)
            k = keys[pl.ds(zo * NX, NX), :, lanes].reshape(256, 128)
            rows = stacked[p]
            products = nt(k, rows)
            capped = jnp.tanh(products[:, :256] * (1.0 / 80.0))
            soft = w * jnp.exp2(capped * (10.0 * LOG2E)) * (1.0 / total[p])
            d_score = soft * (products[:, 256:] - delta[p]) * ((1.0 - capped * capped) * 0.125)
            both = jnp.concatenate([d_score.astype(BF16), soft.astype(BF16)], axis=1)
            d_acc[p] = d_acc[p] + tn(k, both[:, :256])
            grad = nn(both, rows).reshape(NX, NY, 2, 8, 128)
            for side in range(2):
                gsend[zo, :, side, :, lanes] = grad[:, :, side].reshape(NX, 32, 128).astype(BF16)
            return carry

        lax.fori_loop(0, PAIRS, pair, 0)
        ggot[zo, me] = gsend[zo, x, c]
        for j in range(1, 8):
            px, pc = group[j]
            remote(
                gsend.at[zo, px, pc], ggot.at[zo, me], x_send.at[0], x_recv.at[zo],
                dev(y, pc, z, px),
            ).start()

    def gather_tiles(zo):
        pieces = ggot.at[zo, pl.ds(0, 7)]
        remote(pieces, pieces, x_send.at[0], x_recv.at[zo], dev(y, c, z, x)).wait_recv()
        tiles = [asks[zo, s] for s in range(8)]

        def two_tiles(k2, carry):
            sums = []
            for k in range(2):
                value = jnp.zeros((32, D), F32)
                for s in range(8):
                    value = value + ggot[zo, s].astype(F32) * jnp.where(
                        tiles[s] == k2 * 2 + k, 1.0, 0.0
                    )
                sums.append(value.reshape(NY, 1, 8, D))
            joined = jnp.concatenate(sums, axis=1).reshape(NY, 16, D).astype(BF16)
            ysend[zo, :, k2] = joined
            return carry

        lax.fori_loop(0, 4, two_tiles, 0)
        ygot[zo, y] = ysend[zo, y]
        for d in range(1, NY):
            py = (y + d) % NY
            remote(
                ysend.at[zo, py], ygot.at[zo, y], y_send.at[0], y_recv.at[zo],
                dev(py, c, z, x),
            ).start()

    def gather_shards(zo, own):
        pieces = ygot.at[zo, pl.ds(0, 3)]
        remote(pieces, pieces, y_send.at[0], y_recv.at[zo], dev(y, c, z, x)).wait_recv()
        value = ygot[zo, 0].astype(F32)
        for i in range(1, NY):
            value = value + ygot[zo, i].astype(F32)
        zsend[zo] = value.astype(BF16)

        @pl.when(own == 0)
        def _():
            zgot[z] = zsend[z]

        @pl.when(own != 0)
        def _():
            remote(
                zsend.at[zo], zgot.at[z], z_send.at[own], z_recv.at[own], dev(y, c, zo, x)
            ).start()

    def offset(i):
        return (3 * (i + 1)) % NZ

    def body(i, carry):
        @pl.when(i < 8)
        def _():
            compute((z + offset(i)) % NZ)

        @pl.when((i >= 3) & (i < 11))
        def _():
            gather_tiles((z + offset(i - 3)) % NZ)

        @pl.when(i >= 5)
        def _():
            gather_shards((z + offset(i - 5)) % NZ, offset(i - 5))

        return carry

    lax.fori_loop(0, 13, body, 0)
    d_query = jnp.concatenate([unstack_heads(d_acc[p]).T for p in range(PAIRS)], axis=1)
    query_grad[...] = d_rows + d_query
    for d in range(1, NZ):
        remote(zsend.at[0], zgot.at[0], z_send.at[d], z_recv.at[d], dev(y, c, z, x)).wait_recv()
    value = zgot[0].astype(F32)
    for i in range(1, NZ):
        value = value + zgot[i].astype(F32)
    know_grad[...] = value.reshape(8, 8, D)

    pieces = ggot.at[pl.ds(0, 7)]
    remote(pieces, pieces, x_send.at[0], x_recv.at[0], dev(y, c, z, x)).wait_send()
    pieces = ygot.at[pl.ds(0, 6)]
    remote(pieces, pieces, y_send.at[0], y_recv.at[0], dev(y, c, z, x)).wait_send()
    for d in range(1, NZ):
        remote(zsend.at[0], zgot.at[0], z_send.at[d], z_recv.at[d], dev(y, c, z, x)).wait_send()


V = pl.BlockSpec(memory_space=pltpu.VMEM)


def scratch():
    names = dict(
        keys=((32, 64, D), BF16), aug=((Q, D), BF16), mixed_t=((PAIRS, 128, Q), F32),
        total=((PAIRS, 1, 2 * Q), F32), tile_weight=((NZ, 8, Q), F32), onehot=((NZ, Q, 128), BF16),
        facts=((NX, 2, 16, 128), F32), ask_smem=None,
        wanted=((NX, NZ, 128), jnp.int32), asks=((8, NZ, 128), jnp.int32),
        ask_row=((NZ, 128), jnp.int32),
        **{"b%d" % i: ((8, 16, D), BF16) for i in range(16)},
        stage=((8, NZ, 2, 16, D), BF16),
        stacked=((PAIRS, 2 * Q, 128), BF16), acc=((PAIRS, 128, 2 * Q), F32),
        note=((NZ, 24, 128), F32), noted=((NZ, 24, 128), F32), fact=((NX, 2, 16, 128), F32),
    )
    first = [
        pltpu.SMEM((NZ, 128), jnp.int32) if v is None else pltpu.VMEM(*v)
        for v in names.values()
    ]
    first += [
        DMA(n)
        for n in ((2, 4, 4), (2, 4, 4), (1,), (NZ,), (8,), (8,), (NZ,), (NZ,), (NX,), (NX,))
    ] + [DMA]
    second = [
        pltpu.VMEM((Q, D), F32),
        pltpu.VMEM((NZ, Q, D), BF16),
        pltpu.VMEM((NZ, NX, 2, 16, D), BF16),
        pltpu.VMEM((NZ, 2, NX, 16, D), BF16),
        pltpu.VMEM((NZ, 2, NX, 16, D), BF16),
        pltpu.VMEM((NZ, NX, 2, 16, D), BF16),
        pltpu.VMEM((NX, 2, 16, 128), F32),
        pltpu.VMEM((NX, 2, 16, 128), F32),
        pltpu.VMEM((NZ, 2, 64, 512), BF16),
        pltpu.VMEM((Q, 128), F32),
        pltpu.VMEM((NZ, 128), F32),
        pltpu.VMEM((NZ, NZ, 128), F32),
        pltpu.VMEM((2, 4, Q, D), BF16),
        pltpu.VMEM((2, 4, Q, D), BF16),
        pltpu.VMEM((2, 8, 64, D), BF16),
        pltpu.VMEM((2, 8, 64, D), BF16),
    ] + [
        DMA(n)
        for n in (
            (2, 4, 4), (2, 4, 4), (NX, NZ), (NX, NZ), (NX, NZ), (NX, NZ), (NX,), (NX,),
            (2, 4, 2), (2, 4, 2), (NZ,), (NZ,), (2, 8), (2, 8),
        )
    ]
    third = [
        pltpu.VMEM((PAIRS, 4 * Q, 128), BF16),
        pltpu.VMEM((PAIRS, 128, 2 * Q), F32),
        pltpu.VMEM((PAIRS, 1, 2 * Q), F32),
        pltpu.VMEM((NZ, NX, 2, 32, D), BF16),
        pltpu.VMEM((NZ, 8, 32, D), BF16),
        pltpu.VMEM((NZ, NY, 4, 16, D), BF16),
        pltpu.VMEM((NZ, NY, 4, 16, D), BF16),
        pltpu.VMEM((NZ, 4, 16, D), BF16),
        pltpu.VMEM((NZ, 4, 16, D), BF16),
    ] + [DMA(n) for n in ((1,), (NZ,), (1,), (NZ,), (NZ,), (NZ,))]
    return first, second, third


def whole_kernel(*refs):
    sizes = [len(part) for part in scratch()]
    know, numbers, queries, out_proj, labels, loss, query_grad, know_grad, label_step = refs[:9]
    first = refs[9 : 9 + sizes[0]]
    second = refs[9 + sizes[0] : 9 + sizes[0] + sizes[1]]
    third = refs[9 + sizes[0] + sizes[1] :]
    keys, aug, mixed_t, total, tile_weight, onehot, facts, ask_smem = first[:8]
    fact, n_send, n_recv = first[32], first[41], first[42]
    sends = keys_kernel(know, numbers, queries, out_proj, *first)
    d_aug = second[0]
    sends += labels_kernel(
        aug, onehot, facts, fact, n_send, n_recv, labels, d_aug, loss, label_step, *second[1:]
    )
    grads_kernel(
        ask_smem, keys, queries, d_aug, out_proj, mixed_t, total, tile_weight,
        query_grad, know_grad, *third,
    )
    for cp in sends:
        cp.wait_send()


def hand_out(*refs):
    ins, outs, sems = refs[:4], refs[4:8], refs[8]
    copies = [pltpu.make_async_copy(ins[i], outs[i], sems.at[i]) for i in range(4)]
    for cp in copies:
        cp.start()
    for cp in copies:
        cp.wait()


def on_device(queries, tile_ids, knowledge, out_proj, labels, cluster_ids, positive_picks):
    numbers = jnp.concatenate([tile_ids, cluster_ids, positive_picks], axis=1).T
    first, second, third = scratch()
    shapes = [
        jax.ShapeDtypeStruct((1, Q), F32),
        jax.ShapeDtypeStruct((Q, D), F32),
        jax.ShapeDtypeStruct((8, 8, D), F32),
        jax.ShapeDtypeStruct((2, 64, D), F32),
    ]
    results = pl.pallas_call(
        whole_kernel,
        out_shape=shapes,
        in_specs=[V] * 5,
        out_specs=[V] * 4,
        scratch_shapes=first + second + third,
        compiler_params=pltpu.CompilerParams(
            collective_id=1, has_side_effects=True, vmem_limit_bytes=VMEM_LIMIT
        ),
    )(knowledge, numbers, queries, out_proj, labels)
    loss, query_grad, knowledge_grad, label_step = pl.pallas_call(
        hand_out,
        out_shape=shapes,
        in_specs=[V] * 4,
        out_specs=[pl.BlockSpec(memory_space=pl.ANY)] * 4,
        scratch_shapes=[DMA((4,))],
    )(*results)
    return (loss[0], query_grad, knowledge_grad, label_step)


def solution(mesh):
    placed = (
        P(("dp", "table"), None),
        P(("dp", "table"), None),
        P("table", None, None),
        P(),
        P("table", None, None),
        P(("dp", "table"), None),
        P(("dp", "table"), None),
    )
    return jax.shard_map(
        on_device,
        mesh=mesh,
        in_specs=placed,
        out_specs=(
            P(("dp", "table")),
            P(("dp", "table"), None),
            P("table", "dp", None),
            P("table", "dp", None),
        ),
        check_vma=False,
    )
```

```python
import jax
import jax.numpy as jnp
from jax import lax
from jax.experimental import pallas as pl
from jax.experimental.pallas import tpu as pltpu
from jax.sharding import PartitionSpec as P

MESH = pl.DeviceIdType.MESH
DMA = pltpu.SemaphoreType.DMA
F32 = jnp.float32
BF16 = jnp.bfloat16
PAIRS = 6
Q = 128
D = 768
NZ = 8
NX = 4
NY = 4
epsilon = 1e-06
LOG2E = 1.4426950408889634
VMEM_LIMIT = 56 << 20


def where_am_i():
    dp, t = lax.axis_index("dp"), lax.axis_index("table")
    return dp // 2, dp % 2, t // NX, t % NX


def dev(y, c, z, x):
    return (y * 2 + c, z * NX + x)


def greet(peers):
    barrier = pltpu.get_barrier_semaphore()
    for peer in peers:
        pl.semaphore_signal(barrier, inc=1, device_id=peer, device_id_type=MESH)
    return lambda: pl.semaphore_wait(barrier, len(peers))


def remote(src, dst, send, recv, to):
    return pltpu.make_async_remote_copy(
        src_ref=src, dst_ref=dst, send_sem=send, recv_sem=recv, device_id=to, device_id_type=MESH
    )


def nt(a, b):
    return lax.dot_general(a, b, (((1,), (1,)), ((), ())), preferred_element_type=F32)


def tn(a, b):
    return lax.dot_general(a, b, (((0,), (0,)), ((), ())), preferred_element_type=F32)


def nn(a, b):
    return jnp.dot(a, b, preferred_element_type=F32)


def stack_heads(rows, stacked_ref):
    lane = lax.broadcasted_iota(jnp.int32, (Q, 128), 1)
    for p in range(PAIRS):
        part = rows[:, p * 128 : (p + 1) * 128]
        stacked_ref[p, :Q] = jnp.where(lane < 64, part, jnp.zeros_like(part))
        stacked_ref[p, Q:] = jnp.where(lane < 64, jnp.zeros_like(part), part)


def unstack_heads(both):
    return jnp.concatenate([both[0:64, 0:Q], both[64:128, Q : 2 * Q]], axis=0)


def weight_block(tw):
    tw2 = jnp.concatenate([tw, tw], axis=1)
    return jnp.broadcast_to(tw2[:, None, :], (NX, 64, 2 * Q)).reshape(NX * 64, 2 * Q)


XC = [(dx, dc) for dx in range(NX) for dc in range(2)]


def keys_kernel(
    know, numbers, queries, out_proj,
    keys, aug, mixed_t, total, tile_weight, onehot, facts, ask_smem,
    wanted, asks, ask_row,
    half0, half1, r00, r01, r10, r11, r20, r21, l00, l01, l10, l11, l20, l21, far0, far1,
    stage, stacked, acc, note, noted, fact,
    z_send, z_recv, x_send, x_recv, a_send, a_recv, m_send, m_recv, n_send, n_recv, l_sem,
):
    y, c, z, x = where_am_i()
    dp = y * 2 + c
    me = x * 2 + c
    start, far = (half0, half1), (far0, far1)
    r0, r1, r2 = (r00, r01), (r10, r11), (r20, r21)
    l0, l1, l2 = (l00, l01), (l10, l11), (l20, l21)
    right, left = dev(y, c, (z + 1) % NZ, x), dev(y, c, (z + NZ - 1) % NZ, x)
    group = [((x + dx) % NX, (c + dc) % 2) for dx, dc in XC]
    everyone_in = greet(
        [dev(y, pc, z, px) for px, pc in group[1:]]
        + [dev(y, c, (z + d) % NZ, x) for d in range(1, NZ)]
        + [((dp + d) % 8, z * NX + x) for d in range(1, 8)]
    )
    for h in (0, 1):
        start[h][...] = know[:, pl.ds(pl.multiple_of(c * 32 + h * 16, 16), 16), :]
    owner = lax.broadcasted_iota(jnp.int32, (32, Q), 0)
    weight, tile = jnp.zeros((32, Q), F32), jnp.zeros((32, Q), jnp.int32)
    for r in range(4):
        named = numbers[r : r + 1, :]
        hit = (named >> 3) == owner
        weight = weight + jnp.where(hit, 1.0, 0.0)
        tile = jnp.maximum(tile, jnp.where(hit, named & 7, 0))
    tile = jnp.broadcast_to(jnp.max(tile, axis=1, keepdims=True), (32, 128)).reshape(NZ, NX, 128)
    for i in range(NX):
        wanted[i] = tile[:, i]
    ask_copies = []
    asks[me] = wanted[x]
    for zo in range(NZ):
        tile_weight[zo, 0:NX] = weight[zo * NX : zo * NX + NX]
    everyone_in()
    for j in range(1, 8):
        px, pc = group[j]
        cp = remote(wanted.at[px], asks.at[me], a_send.at[j], a_recv.at[j], dev(y, pc, z, px))
        cp.start()
        ask_copies.append(cp)
    ring = {}
    slots = ((start, r0, r1, r2, far), (start, l0, l1, l2, far))

    def ring_send(way, step, k):
        h, piece = k // 2, pl.ds((k % 2) * 4, 4)
        cp = remote(
            slots[way][step][h].at[piece], slots[way][step + 1][h].at[piece],
            z_send.at[way, step, k], z_recv.at[way, step, k], right if way == 0 else left,
        )
        cp.start()
        ring[way, step, k] = cp

    for k in range(4):
        for way in (0, 1):
            ring_send(way, 0, k)
    cluster = lax.broadcasted_iota(jnp.int32, (64, Q), 0)
    ids = [numbers[4 + i : 5 + i, :] for i in range(4)]
    member = ids[0] == cluster
    for i in range(1, 4):
        member = member | (ids[i] == cluster)
    row = lax.broadcasted_iota(jnp.int32, (Q, 128), 0)
    lane = lax.broadcasted_iota(jnp.int32, (Q, 128), 1)
    before = jnp.where(row < lane, 1.0, 0.0).astype(BF16)
    rank = nn(jnp.where(member, 1.0, 0.0).astype(BF16), before)
    rank = jnp.where(member, rank, -1.0)
    picks = [numbers[8 + j : 9 + j, :] for j in range(4)]
    columns = []
    for j in range(4):
        column = picks[j] >> 9
        named = jnp.where(column == 0, ids[0], 0)
        for i in range(1, 4):
            named = jnp.where(column == i, ids[i], named)
        columns.append(named)
    columns += [(pick & 511) >> 8 for pick in picks] + [pick & 255 for pick in picks]
    columns += [jnp.ones_like(picks[0])] + [jnp.zeros_like(picks[0])] * 3
    columns = jnp.concatenate(columns, axis=0).astype(F32)
    for i in range(NZ):
        note[i, 0:8] = rank[i * 8 : i * 8 + 8]
        note[i, 8:24] = columns
    stack_heads(queries[...], stacked)
    acc[...] = jnp.zeros_like(acc)
    total[...] = jnp.zeros_like(total)
    note_copies = []
    for d in range(1, NZ):
        zp = (z + d) % NZ
        cp = remote(
            note.at[zp], noted.at[NZ - d], m_send.at[d], m_recv.at[NZ - d], dev(y, c, zp, x)
        )
        cp.start()
        note_copies.append(cp)
    noted[0] = note[z]

    def slots_and_facts():
        for d in range(1, NZ):
            remote(note.at[0], noted.at[d], m_send.at[d], m_recv.at[d], right).wait_recv()
        spread = jnp.where(
            lax.broadcasted_iota(jnp.int32, (16, 128), 0)
            == lax.broadcasted_iota(jnp.int32, (16, 128), 1) // 16,
            1.0, 0.0,
        ).astype(BF16)
        place = (lane % 16).astype(F32)
        about = noted[:, 8:24, :].reshape(128, Q).T
        value = jnp.zeros((128, 128), F32)
        for o in range(NZ):
            hot = jnp.where(tn(noted[o, 0:16].astype(BF16), spread) == place, 1.0, 0.0).astype(BF16)
            onehot[o] = hot
            value = value + tn(hot, jnp.where(lane // 16 == o, about, 0.0).astype(BF16))
        fact[...] = value.reshape(NX, 2, 16, 128)
        facts[x] = fact[x]
        for dx in range(1, NX):
            px = (x + dx) % NX
            cp = remote(fact.at[px], facts.at[x], n_send.at[dx], n_recv.at[dx], dev(y, c, z, px))
            cp.start()
            note_copies.append(cp)

    for cp in ask_copies:
        cp.wait()
    peer = lax.broadcasted_iota(jnp.int32, (NZ, 128), 1)
    table = jnp.zeros((NZ, 128), jnp.int32)
    for i in range(8):
        table = jnp.where(peer == i, asks[i], table)
    ask_row[...] = table
    cp = pltpu.make_async_copy(ask_row, ask_smem, l_sem)
    cp.start()
    cp.wait()

    def serve(zo, h, shard):
        row = pl.ds(pl.multiple_of(c * 32 + h * 16, 16), 16)
        for j, (px, pc) in enumerate(group):
            tile = jnp.clip(ask_smem[zo, px * 2 + pc], 0, 7)
            if j == 0:
                keys[zo * NX + x, row] = shard[tile]
                continue
            stage[j, zo, h] = shard[tile]
            cp = remote(
                stage.at[j, zo, h], keys.at[zo * NX + x, row], x_send.at[0],
                x_recv.at[zo], dev(y, pc, z, px),
            )
            cp.start()

    def arrived(zo):
        pieces = stage.at[pl.ds(0, 7), zo]
        remote(pieces, pieces, x_send.at[0], x_recv.at[zo], right).wait_recv()

    def attend(zo):
        w = weight_block(tile_weight[zo, 0:NX])

        def pair(p, carry):
            lanes = pl.ds(pl.multiple_of(p * 128, 128), 128)
            k = keys[pl.ds(zo * NX, NX), :, lanes].reshape(256, 128)
            capped = jnp.tanh(nt(k, stacked[p]) * (1.0 / 80.0))
            raw = w * jnp.exp2(capped * (10.0 * LOG2E))
            total[p] = total[p] + jnp.sum(raw, axis=0, keepdims=True)
            acc[p] = acc[p] + tn(k, raw.astype(BF16))
            return carry

        lax.fori_loop(0, PAIRS, pair, 0, unroll=2)

    def wait_step(way, step, k):
        ring[way, step, k].wait_recv()

    for h in (0, 1):
        serve(z, h, start[h])
    pending = [z]
    for step in range(1, 4):
        fresh = [(z + NZ - step) % NZ, (z + step) % NZ]
        for h in (0, 1):
            for k in (2 * h, 2 * h + 1):
                for way in (0, 1):
                    wait_step(way, step - 1, k)
                    if step < 3 or (k < 2) == (way == 0):
                        ring_send(way, step, k)
            for way in (0, 1):
                serve(fresh[way], h, slots[way][step][h])
        for zo in pending:
            arrived(zo)
            attend(zo)
        if step == 1:
            slots_and_facts()
        pending = fresh
    for h in (0, 1):
        for k in (2 * h, 2 * h + 1):
            wait_step(h, 3, k)
        serve((z + 4) % NZ, h, far[h])
    for zo in pending:
        arrived(zo)
        attend(zo)
    arrived((z + 4) % NZ)
    attend((z + 4) % NZ)
    for p in range(PAIRS):
        mixed_t[p] = unstack_heads(acc[p] / total[p])
    mixed = jnp.concatenate([mixed_t[p].T for p in range(PAIRS)], axis=1).astype(BF16)
    aug[...] = (queries[...].astype(F32) + nn(mixed, out_proj[...])).astype(BF16)
    pieces = stage.at[pl.ds(0, 7)]
    return list(ring.values()) + [remote(pieces, pieces, x_send.at[0], x_recv.at[0], right)] + note_copies


def labels_kernel(
    aug, onehot, facts, fact, n_send, n_recv, labels,
    d_aug, loss, label_step,
    rows, served, got, back, back_got, lstage, lgot, dlogit, lpart, lsend, lrecv,
    psend, prbuf, label_grad, label_got,
    z_send, z_recv, x_send, x_recv, b_send, b_recv, s_send, s_recv, p_send, p_recv, q_send, q_recv,
    g_send, g_recv,
):
    y, c, z, x = where_am_i()
    dp = y * 2 + c
    right, left = dev(y, c, (z + 1) % NZ, x), dev(y, c, (z + NZ - 1) % NZ, x)
    ring = {}

    def ring_send(way, step, k):
        own = (z + NZ - step) % NZ if way == 0 else (z + step) % NZ
        piece = pl.ds(k * 32, 32)
        src = aug.at[piece] if step == 0 else rows.at[own, piece]
        cp = remote(
            src, rows.at[own, piece], z_send.at[way, step, k], z_recv.at[way, step, k],
            right if way == 0 else left,
        )
        cp.start()
        ring[way, step, k] = cp

    for k in range(4):
        for way in (0, 1):
            ring_send(way, 0, k)
    rows[z] = aug[...]
    sent = []

    def serve(o):
        zs = (z + o) % NZ
        picked = tn(onehot[o], rows[zs]).astype(BF16)
        served[zs] = picked.reshape(NX, 2, 16, D)
        got[zs, :, x] = served[zs, x]
        for dx in range(1, NX):
            px = (x + dx) % NX
            cp = remote(
                served.at[zs, px], got.at[zs, :, x], x_send.at[dx, zs], x_recv.at[dx, zs],
                dev(y, c, z, px),
            )
            cp.start()
            sent.append(cp)

    label = lax.broadcasted_iota(jnp.int32, (64, 512), 1).astype(F32)
    lane = lax.broadcasted_iota(jnp.int32, (NX, 16, 128), 2)
    lstage[...] = jnp.zeros_like(lstage)

    def work(o):
        zs = (z + o) % NZ
        for dx in range(1, NX):
            remote(
                served.at[0, 0], got.at[zs, :, 0], x_send.at[dx, zs], x_recv.at[dx, zs], right
            ).wait_recv()

        def cluster(cl, carry):
            entries = got[zs, cl].reshape(64, D)
            logits = nt(entries, labels[cl])
            want = facts[:, cl].reshape(64, 128)
            first = o * 16
            live = want[:, first + 12 : first + 13]
            cluster_id = ((z * NX + x) * 2 + cl).astype(F32)
            hit = None
            for j in range(4):
                named = want[:, first + j : first + j + 1]
                high = want[:, first + 4 + j : first + 5 + j]
                low = want[:, first + 8 + j : first + 9 + j]
                one = label == jnp.where(named == cluster_id, high * 256.0 + low, -1.0)
                hit = one if hit is None else hit | one
            e = jnp.exp(-jnp.abs(logits))
            soft = jnp.maximum(logits, 0.0) + jnp.log1p(e)
            pair_loss = jnp.sum(soft - jnp.where(hit, logits, 0.0), axis=1, keepdims=True) * live
            inv = 1.0 / (1.0 + e)
            sig = jnp.where(logits >= 0, inv, 1.0 - inv)
            dl = ((sig - jnp.where(hit, 1.0, 0.0)) * live).astype(BF16)
            dlogit[zs, cl] = dl
            back[zs, cl] = nn(dl, labels[cl]).astype(BF16).reshape(NX, 16, D)
            spread = jnp.broadcast_to(pair_loss, (64, 128)).reshape(NX, 16, 128)
            lstage[:, cl] = jnp.where(lane == zs, spread, lstage[:, cl])
            return carry

        lax.fori_loop(0, 2, cluster, 0)

    def send_back(zs):
        back_got[zs, x] = back[zs, :, x]
        for dx in range(1, NX):
            px = (x + dx) % NX
            cp = remote(
                back.at[zs, :, px], back_got.at[zs, x], b_send.at[dx, zs], b_recv.at[dx, zs],
                dev(y, c, z, px),
            )
            cp.start()
            sent.append(cp)

    serve(0)
    for dx in range(1, NX):
        remote(fact.at[0], facts.at[0], n_send.at[dx], n_recv.at[dx], right).wait_recv()
    pending = [0]
    for step in range(1, 4):
        for k in range(4):
            for way in (0, 1):
                ring[way, step - 1, k].wait_recv()
                if step < 3 or (k < 2) == (way == 0):
                    ring_send(way, step, k)
        fresh = [NZ - step, step]
        for o in fresh:
            serve(o)
        for o in pending:
            work(o)
        pending = fresh
    for k in range(4):
        ring[0 if k < 2 else 1, 3, k].wait_recv()
    serve(4)
    for o in pending:
        work(o)
        send_back((z + o) % NZ)
    work(4)
    for d in (4, 2, 6, 1, 7, 0):
        send_back((z + d) % NZ)
    loss_copies = []
    for dx in range(1, NX):
        px = (x + dx) % NX
        cp = remote(lstage.at[px], lgot.at[x], s_send.at[dx], s_recv.at[dx], dev(y, c, z, px))
        cp.start()
        loss_copies.append(cp)
    lgot[x] = lstage[x]

    def partial(o):
        zs = (z + o) % NZ
        for dx in range(1, NX):
            remote(
                back.at[0, :, 0], back_got.at[zs, 0], b_send.at[dx, zs], b_recv.at[dx, zs], right
            ).wait_recv()
        return nn(onehot[o], back_got[zs].reshape(128, D))

    label_copies = []

    def label_part(cl):
        entries = got[:, cl].reshape(512, D)
        for part in range(2):
            columns = slice(part * 256, part * 256 + 256)
            value = tn(dlogit[:, cl, :, columns].reshape(512, 256), entries)
            label_grad[cl, part * 4 : part * 4 + 4] = value.astype(BF16).reshape(4, 64, D)
        label_got[cl, dp] = label_grad[cl, dp]
        for d in range(1, 8):
            to = (dp + d) % 8
            cp = remote(
                label_grad.at[cl, to], label_got.at[cl, dp], g_send.at[cl, d], g_recv.at[cl, d],
                (to, z * NX + x),
            )
            cp.start()
            label_copies.append(cp)

    p_copies = {}

    def chain_send(way, step, h, value):
        piece = pl.ds(h * 64, 64)
        psend[way, step, piece] = value.astype(BF16)
        cp = remote(
            psend.at[way, step, piece], prbuf.at[way, step, piece],
            p_send.at[way, step, h], p_recv.at[way, step, h], right if way == 0 else left,
        )
        cp.start()
        p_copies[way, step, h] = cp

    label_part(0)
    far = partial(4)
    for way in (0, 1):
        chain_send(way, 0, way, far[way * 64 : way * 64 + 64])
    label_part(1)
    for step in range(1, 4):
        d = 4 - step
        own = [partial(d), partial(NZ - d)]
        for h in (0, 1):
            for way in (h, 1 - h):
                value = own[way][h * 64 : h * 64 + 64]
                if (way, step - 1, h) in p_copies:
                    p_copies[way, step - 1, h].wait_recv()
                    value = value + prbuf[way, step - 1, h * 64 : h * 64 + 64].astype(F32)
                chain_send(way, step, h, value)
    mine = partial(0)
    for cp in loss_copies:
        cp.wait()
    losses = jnp.concatenate([lgot[i].reshape(32, 128) for i in range(NX)], axis=0).astype(BF16)
    out_lane = lax.broadcasted_iota(jnp.int32, (Q, 128), 1)
    lpart[...] = jnp.zeros_like(lpart)

    def loss_of(i, carry):
        lpart[...] = lpart[...] + jnp.where(out_lane == (z + i) % NZ, nn(onehot[i], losses), 0.0)
        return carry

    lax.fori_loop(0, NZ, loss_of, 0)
    lsend[...] = lpart[...].T[:NZ]
    l_copies = []
    for d in range(1, NZ):
        zp = (z + d) % NZ
        cp = remote(lsend, lrecv.at[z], q_send.at[d], q_recv.at[d], dev(y, c, zp, x))
        cp.start()
        l_copies.append(cp)
    lrecv[z] = lsend[...]
    for h in (0, 1):
        for way in (0, 1):
            p_copies[way, 3, h].wait_recv()
    d_aug[...] = mine + prbuf[0, 3].astype(F32) + prbuf[1, 3].astype(F32)
    for cp in l_copies:
        cp.wait()
    loss[...] = jnp.sum(lrecv[:, pl.ds(z, 1), :], axis=0) * (1.0 / 2048.0)
    for cp in label_copies:
        cp.wait()
    for cl in range(2):
        grad = label_got[cl, 0].astype(F32)
        for i in range(1, 8):
            grad = grad + label_got[cl, i].astype(F32)
        square = jnp.mean(grad * grad, axis=1, keepdims=True)
        label_step[cl] = grad * lax.rsqrt(square + epsilon)
    return list(p_copies.values()) + list(ring.values()) + sent


def grads_kernel(
    asks, keys, queries, d_aug, out_proj, mixed_t, total, tile_weight,
    query_grad, know_grad,
    stacked, d_acc, delta, gsend, ggot, ysend, ygot, zsend, zgot,
    x_send, x_recv, y_send, y_recv, z_send, z_recv,
):
    y, c, z, x = where_am_i()
    me = x * 2 + c
    group = [((x + dx) % NX, (c + dc) % 2) for dx, dc in XC]
    d_rows = d_aug[...]
    back_proj = nt(d_rows.astype(BF16), out_proj[...]).astype(BF16)
    stack_heads(queries[...], stacked.at[:, 0:256])
    stack_heads(back_proj, stacked.at[:, 256:512])
    for p in range(PAIRS):
        product = mixed_t[p] * back_proj[:, p * 128 : (p + 1) * 128].astype(F32).T
        delta[p] = jnp.concatenate(
            [
                jnp.sum(product[:64], axis=0, keepdims=True),
                jnp.sum(product[64:], axis=0, keepdims=True),
            ],
            axis=1,
        )
    d_acc[...] = jnp.zeros_like(d_acc)

    def compute(zo):
        w = weight_block(tile_weight[zo, 0:NX])

        def pair(p, carry):
            lanes = pl.ds(pl.multiple_of(p * 128, 128), 128)
            k = keys[pl.ds(zo * NX, NX), :, lanes].reshape(256, 128)
            rows = stacked[p]
            products = nt(k, rows)
            capped = jnp.tanh(products[:, :256] * (1.0 / 80.0))
            soft = w * jnp.exp2(capped * (10.0 * LOG2E)) * (1.0 / total[p])
            d_score = soft * (products[:, 256:] - delta[p]) * ((1.0 - capped * capped) * 0.125)
            both = jnp.concatenate([d_score.astype(BF16), soft.astype(BF16)], axis=1)
            d_acc[p] = d_acc[p] + tn(k, both[:, :256])
            grad = nn(both, rows).reshape(NX, NY, 2, 8, 128)
            for side in range(2):
                gsend[zo, :, side, :, lanes] = grad[:, :, side].reshape(NX, 32, 128).astype(BF16)
            return carry

        lax.fori_loop(0, PAIRS, pair, 0, unroll=2)
        ggot[zo, me] = gsend[zo, x, c]
        for j in range(1, 8):
            px, pc = group[j]
            remote(
                gsend.at[zo, px, pc], ggot.at[zo, me], x_send.at[0], x_recv.at[zo],
                dev(y, pc, z, px),
            ).start()

    def gather_tiles(zo):
        pieces = ggot.at[zo, pl.ds(0, 7)]
        remote(pieces, pieces, x_send.at[0], x_recv.at[zo], dev(y, c, z, x)).wait_recv()
        tiles = [asks[zo, s] for s in range(8)]

        def two_tiles(k2, carry):
            sums = []
            for k in range(2):
                value = jnp.zeros((32, D), F32)
                for s in range(8):
                    value = value + ggot[zo, s].astype(F32) * jnp.where(
                        tiles[s] == k2 * 2 + k, 1.0, 0.0
                    )
                sums.append(value.reshape(NY, 1, 8, D))
            joined = jnp.concatenate(sums, axis=1).reshape(NY, 16, D).astype(BF16)
            ysend[zo, :, k2] = joined
            return carry

        lax.fori_loop(0, 4, two_tiles, 0)
        ygot[zo, y] = ysend[zo, y]
        for d in range(1, NY):
            py = (y + d) % NY
            remote(
                ysend.at[zo, py], ygot.at[zo, y], y_send.at[0], y_recv.at[zo],
                dev(py, c, z, x),
            ).start()

    def gather_shards(zo, own):
        pieces = ygot.at[zo, pl.ds(0, 3)]
        remote(pieces, pieces, y_send.at[0], y_recv.at[zo], dev(y, c, z, x)).wait_recv()
        value = ygot[zo, 0].astype(F32)
        for i in range(1, NY):
            value = value + ygot[zo, i].astype(F32)
        zsend[zo] = value.astype(BF16)

        @pl.when(own == 0)
        def _():
            zgot[z] = zsend[z]

        @pl.when(own != 0)
        def _():
            remote(
                zsend.at[zo], zgot.at[z], z_send.at[own], z_recv.at[own], dev(y, c, zo, x)
            ).start()

    def offset(i):
        return (3 * (i + 1)) % NZ

    def body(i, carry):
        @pl.when(i < 8)
        def _():
            compute((z + offset(i)) % NZ)

        @pl.when((i >= 2) & (i < 10))
        def _():
            gather_tiles((z + offset(i - 2)) % NZ)

        @pl.when((i >= 4) & (i < 12))
        def _():
            gather_shards((z + offset(i - 4)) % NZ, offset(i - 4))

        return carry

    lax.fori_loop(0, 12, body, 0)
    d_query = jnp.concatenate([unstack_heads(d_acc[p]).T for p in range(PAIRS)], axis=1)
    query_grad[...] = d_rows + d_query
    for d in range(1, NZ):
        remote(zsend.at[0], zgot.at[0], z_send.at[d], z_recv.at[d], dev(y, c, z, x)).wait_recv()
    value = zgot[0].astype(F32)
    for i in range(1, NZ):
        value = value + zgot[i].astype(F32)
    know_grad[...] = value.reshape(8, 8, D)

    pieces = ggot.at[pl.ds(0, 7)]
    remote(pieces, pieces, x_send.at[0], x_recv.at[0], dev(y, c, z, x)).wait_send()
    pieces = ygot.at[pl.ds(0, 6)]
    remote(pieces, pieces, y_send.at[0], y_recv.at[0], dev(y, c, z, x)).wait_send()
    for d in range(1, NZ):
        remote(zsend.at[0], zgot.at[0], z_send.at[d], z_recv.at[d], dev(y, c, z, x)).wait_send()


V = pl.BlockSpec(memory_space=pltpu.VMEM)


def scratch():
    names = dict(
        keys=((32, 64, D), BF16), aug=((Q, D), BF16), mixed_t=((PAIRS, 128, Q), F32),
        total=((PAIRS, 1, 2 * Q), F32), tile_weight=((NZ, 8, Q), F32), onehot=((NZ, Q, 128), BF16),
        facts=((NX, 2, 16, 128), F32), ask_smem=None,
        wanted=((NX, NZ, 128), jnp.int32), asks=((8, NZ, 128), jnp.int32),
        ask_row=((NZ, 128), jnp.int32),
        **{"b%d" % i: ((8, 16, D), BF16) for i in range(16)},
        stage=((8, NZ, 2, 16, D), BF16),
        stacked=((PAIRS, 2 * Q, 128), BF16), acc=((PAIRS, 128, 2 * Q), F32),
        note=((NZ, 24, 128), F32), noted=((NZ, 24, 128), F32), fact=((NX, 2, 16, 128), F32),
    )
    first = [
        pltpu.SMEM((NZ, 128), jnp.int32) if v is None else pltpu.VMEM(*v)
        for v in names.values()
    ]
    first += [
        DMA(n)
        for n in ((2, 4, 4), (2, 4, 4), (1,), (NZ,), (8,), (8,), (NZ,), (NZ,), (NX,), (NX,))
    ] + [DMA]
    second = [
        pltpu.VMEM((Q, D), F32),
        pltpu.VMEM((NZ, Q, D), BF16),
        pltpu.VMEM((NZ, NX, 2, 16, D), BF16),
        pltpu.VMEM((NZ, 2, NX, 16, D), BF16),
        pltpu.VMEM((NZ, 2, NX, 16, D), BF16),
        pltpu.VMEM((NZ, NX, 2, 16, D), BF16),
        pltpu.VMEM((NX, 2, 16, 128), F32),
        pltpu.VMEM((NX, 2, 16, 128), F32),
        pltpu.VMEM((NZ, 2, 64, 512), BF16),
        pltpu.VMEM((Q, 128), F32),
        pltpu.VMEM((NZ, 128), F32),
        pltpu.VMEM((NZ, NZ, 128), F32),
        pltpu.VMEM((2, 4, Q, D), BF16),
        pltpu.VMEM((2, 4, Q, D), BF16),
        pltpu.VMEM((2, 8, 64, D), BF16),
        pltpu.VMEM((2, 8, 64, D), BF16),
    ] + [
        DMA(n)
        for n in (
            (2, 4, 4), (2, 4, 4), (NX, NZ), (NX, NZ), (NX, NZ), (NX, NZ), (NX,), (NX,),
            (2, 4, 2), (2, 4, 2), (NZ,), (NZ,), (2, 8), (2, 8),
        )
    ]
    third = [
        pltpu.VMEM((PAIRS, 4 * Q, 128), BF16),
        pltpu.VMEM((PAIRS, 128, 2 * Q), F32),
        pltpu.VMEM((PAIRS, 1, 2 * Q), F32),
        pltpu.VMEM((NZ, NX, 2, 32, D), BF16),
        pltpu.VMEM((NZ, 8, 32, D), BF16),
        pltpu.VMEM((NZ, NY, 4, 16, D), BF16),
        pltpu.VMEM((NZ, NY, 4, 16, D), BF16),
        pltpu.VMEM((NZ, 4, 16, D), BF16),
        pltpu.VMEM((NZ, 4, 16, D), BF16),
    ] + [DMA(n) for n in ((1,), (NZ,), (1,), (NZ,), (NZ,), (NZ,))]
    return first, second, third


def whole_kernel(*refs):
    sizes = [len(part) for part in scratch()]
    know, numbers, queries, out_proj, labels, loss, query_grad, know_grad, label_step = refs[:9]
    first = refs[9 : 9 + sizes[0]]
    second = refs[9 + sizes[0] : 9 + sizes[0] + sizes[1]]
    third = refs[9 + sizes[0] + sizes[1] :]
    keys, aug, mixed_t, total, tile_weight, onehot, facts, ask_smem = first[:8]
    fact, n_send, n_recv = first[32], first[41], first[42]
    sends = keys_kernel(know, numbers, queries, out_proj, *first)
    d_aug = second[0]
    sends += labels_kernel(
        aug, onehot, facts, fact, n_send, n_recv, labels, d_aug, loss, label_step, *second[1:]
    )
    grads_kernel(
        ask_smem, keys, queries, d_aug, out_proj, mixed_t, total, tile_weight,
        query_grad, know_grad, *third,
    )
    for cp in sends:
        cp.wait_send()


def hand_out(*refs):
    ins, outs, sems = refs[:4], refs[4:8], refs[8]
    copies = [pltpu.make_async_copy(ins[i], outs[i], sems.at[i]) for i in range(4)]
    for cp in copies:
        cp.start()
    for cp in copies:
        cp.wait()


def on_device(queries, tile_ids, knowledge, out_proj, labels, cluster_ids, positive_picks):
    numbers = jnp.concatenate([tile_ids, cluster_ids, positive_picks], axis=1).T
    first, second, third = scratch()
    shapes = [
        jax.ShapeDtypeStruct((1, Q), F32),
        jax.ShapeDtypeStruct((Q, D), F32),
        jax.ShapeDtypeStruct((8, 8, D), F32),
        jax.ShapeDtypeStruct((2, 64, D), F32),
    ]
    results = pl.pallas_call(
        whole_kernel,
        out_shape=shapes,
        in_specs=[V] * 5,
        out_specs=[V] * 4,
        scratch_shapes=first + second + third,
        compiler_params=pltpu.CompilerParams(
            collective_id=1, has_side_effects=True, vmem_limit_bytes=VMEM_LIMIT
        ),
    )(knowledge, numbers, queries, out_proj, labels)
    loss, query_grad, knowledge_grad, label_step = pl.pallas_call(
        hand_out,
        out_shape=shapes,
        in_specs=[V] * 4,
        out_specs=[pl.BlockSpec(memory_space=pl.ANY)] * 4,
        scratch_shapes=[DMA((4,))],
    )(*results)
    return (loss[0], query_grad, knowledge_grad, label_step)


def solution(mesh):
    placed = (
        P(("dp", "table"), None),
        P(("dp", "table"), None),
        P("table", None, None),
        P(),
        P("table", None, None),
        P(("dp", "table"), None),
        P(("dp", "table"), None),
    )
    return jax.shard_map(
        on_device,
        mesh=mesh,
        in_specs=placed,
        out_specs=(
            P(("dp", "table")),
            P(("dp", "table"), None),
            P("table", "dp", None),
            P("table", "dp", None),
        ),
        check_vma=False,
    )
```
